256 devices in a mesh: pipe: 8 (over x, core), expert: 32 (over z, y).
Axes of the slice: x: 4, y: 4, z: 8, core: 2. Of those that a mesh axis runs over, the one named last changes fastest.
Arguments:
- forward_in: bfloat16 [8, 4096, 3584], P('pipe', 'expert'), may hold values from -6 to 6
- forward_route: int32 [8, 4096, 1], P('pipe', 'expert'), may hold values from 0 to 7; in each aligned block of 128 rows (0 to 127, 128 to 255, ..., all dimensions but the last counted through in order) at most 20 rows name the same one
- forward_share: float32 [8, 4096, 1], P('pipe', 'expert'), may hold values from 0.2 to 1
- backward_in: bfloat16 [8, 4096, 3584], P('pipe', 'expert'), may hold values from -6 to 6
- backward_grad: bfloat16 [8, 4096, 3584], P('pipe', 'expert'), may hold values from -6 to 6
- backward_route: int32 [8, 4096, 1], P('pipe', 'expert'), may hold values from 0 to 7; in each aligned block of 128 rows (0 to 127, 128 to 255, ..., all dimensions but the last counted through in order) at most 20 rows name the same one
- backward_share: float32 [8, 4096, 1], P('pipe', 'expert'), may hold values from 0.2 to 1
- norm_gain: float32 [8, 3584], P('pipe'), may hold values from 0.25 to 1.75
- gate_matrix: bfloat16 [8, 3584, 8192], P('pipe', None, 'expert'), may hold values from -0.09375 to 0.09375
- up_matrix: bfloat16 [8, 3584, 8192], P('pipe', None, 'expert'), may hold values from -0.09375 to 0.09375
- down_matrix: bfloat16 [8, 8192, 3584], P('pipe', 'expert'), may hold values from -0.1875 to 0.1875
Outputs:
- next_forward: bfloat16 [8, 4096, 3584], P('pipe', 'expert')
- next_backward: bfloat16 [8, 4096, 3584], P('pipe', 'expert')
The draws below stay inside these ranges and needn't reach their ends.
Inputs may be any that keep to these rules, and one draw needn't show every extreme that they name: `forward_route`: each row names exactly one expert of its section. Among the rows of one device (aligned blocks of 128 rows) no expert is named more than 20 times, a bound that some block reaches. `backward_route`: as for forward_route.
All inputs are finite; a program needn't handle non-finite values.
Results may differ from the reference program's by a relative error of at most 0.0058.
Values may be sent and summed in bfloat16 or wider, within the bound.
A program may use at most 128 MiB of HBM per device.

```python
import math
import jax
import jax.numpy as jnp
import numpy as np
from jax import lax

D = 3584
FFE = 1024
SLICES = 4
TOPK = 1
TOK_DEV = 128
H_DEV = 256
EXPERTS = 8
CAP = 20
TOKENS = 4096
N_PIPE = 8
N_EXPERT = 32


def block_scale(own_key, shape, pieces, smallest, top_value):
    level = 1.0
    for dim, blocks in pieces:
        steps = jax.random.uniform(jax.random.fold_in(jax.random.fold_in(own_key, 6), dim), (blocks,), jnp.float32, smallest / len(pieces), top_value / len(pieces))
        level = level * jnp.repeat(jnp.exp(steps), shape[dim] // blocks).reshape((-1,) + (1,) * (len(shape) - 1 - dim))
    return level


def assign_block(stream_key, own, number, rows, number_of, top, bound, lean):
    order = jax.random.permutation(stream_key, number_of)
    crowded, common = load_shares(number_of, rows * top, bound, lean, True), load_shares(number_of, rows * top, bound, lean, False)
    places = jnp.arange(number_of)

    def named(lengths, turn):
        used = int((lengths > 0).sum())
        fixed = max(1, used // 4)
        moved = fixed + (places - fixed + turn * (used - fixed)) % max(1, number_of - fixed)
        return jnp.zeros((number_of,), jnp.int32).at[order[jnp.where(places < fixed, places, moved)]].set(jnp.asarray(lengths, jnp.int32))

    lengths = jnp.where(number % 4 == 0, named(crowded, number // 4), named(common, number - number // 4 - 1))
    mixed = jax.random.permutation(jax.random.fold_in(own, 3), number_of)
    donor, sink = mixed[0:number_of // 2 * 2:2], mixed[1:number_of // 2 * 2:2]
    slack = jnp.minimum(lengths[donor] - 1, bound - lengths[sink]) // 2
    slack = jnp.where((donor == order[0]) | (sink == order[0]) | (lengths[sink] == 0), 0, jnp.maximum(slack, 0))
    moved = jax.random.randint(jax.random.fold_in(own, 4), (number_of // 2,), 0, 1 << 20) % (slack + 1)
    lengths = lengths.at[donor].add(-moved).at[sink].add(moved)
    items = jnp.searchsorted(jnp.cumsum(lengths), jnp.arange(rows * top), side="right").astype(jnp.int32)
    listing = items.reshape(top, rows).T
    listing = listing[jax.random.permutation(jax.random.fold_in(own, 1), rows)]
    turn = jax.random.randint(jax.random.fold_in(own, 2), (rows, 1), 0, top)
    return jnp.take_along_axis(listing, (jnp.arange(top)[None, :] + turn) % top, axis=1)


def load_shares(amount, total, bound, lean, full):
    weights = [(1 << 20) // math.isqrt(rank ** lean) + 1 for rank in range(1, amount + 1)]
    largest = bound if full else min(bound, max(-(-total // amount), total * weights[0] // sum(weights)))
    least = 1 if total - largest >= amount - 1 else 0
    given, surplus = [largest] + [least] * (amount - 1), total - largest - least * (amount - 1)
    while surplus > 0:
        candidates = [i for i in range(1, amount) if given[i] < largest] or [i for i in range(1, amount) if given[i] < bound]
        whole, remaining = sum([weights[i] for i in candidates]), surplus
        for i in candidates:
            addition = min(bound - given[i], max(1, remaining * weights[i] // whole), surplus)
            given[i] = given[i] + addition
            surplus = surplus - addition
    return np.array(given)


def gaussian(rng, shape, deviation, bound, pieces=(), kind=jnp.bfloat16):
    loudness = block_scale(rng, shape, pieces, -0.22, 0.18) if pieces else 1.0
    array = jax.random.normal(rng, shape, jnp.float32) * deviation * loudness
    return jnp.minimum(jnp.maximum(array, -bound), bound).astype(kind)


def setup_inputs(seed: int = 0) -> dict:
    keys = jax.random.split(jax.random.key(seed), 12)
    forward_in = gaussian(keys[0], (N_PIPE, TOKENS, D), 1.0, 6.0, ((0, 8), (1, 32)))
    forward_route_keys = jax.random.split(jax.random.fold_in(keys[1], 1), N_PIPE * TOKENS // TOK_DEV)
    forward_route_turns = jax.random.permutation(jax.random.fold_in(keys[1], 3), N_PIPE * TOKENS // TOK_DEV)
    forward_route = jax.vmap(lambda own, number: assign_block(jax.random.fold_in(keys[1], 2), own, number, TOK_DEV, EXPERTS, TOPK, CAP, 2))(forward_route_keys, forward_route_turns).reshape((N_PIPE, TOKENS, TOPK))
    forward_share = jnp.clip(0.2 + 0.8 * jax.random.uniform(keys[2], (N_PIPE, TOKENS, TOPK), jnp.float32) ** block_scale(keys[2], (N_PIPE, TOKENS, TOPK), ((0, 8), (1, 32)), -0.2, 0.2), 0.2, 1.0)
    backward_in = gaussian(keys[3], (N_PIPE, TOKENS, D), 1.0, 6.0, ((0, 8), (1, 32)))
    backward_grad = gaussian(keys[4], (N_PIPE, TOKENS, D), 1.0, 6.0, ((0, 8), (1, 32)))
    backward_route_keys = jax.random.split(jax.random.fold_in(keys[5], 1), N_PIPE * TOKENS // TOK_DEV)
    backward_route_turns = jax.random.permutation(jax.random.fold_in(keys[5], 3), N_PIPE * TOKENS // TOK_DEV)
    backward_route = jax.vmap(lambda own, number: assign_block(jax.random.fold_in(keys[5], 2), own, number, TOK_DEV, EXPERTS, TOPK, CAP, 2))(backward_route_keys, backward_route_turns).reshape((N_PIPE, TOKENS, TOPK))
    backward_share = jnp.clip(0.2 + 0.8 * jax.random.uniform(keys[6], (N_PIPE, TOKENS, TOPK), jnp.float32) ** block_scale(keys[6], (N_PIPE, TOKENS, TOPK), ((0, 8), (1, 32)), -0.2, 0.2), 0.2, 1.0)
    norm_gain = jnp.clip(1.0 + 0.15 * jax.random.normal(keys[7], (N_PIPE, D), jnp.float32), 0.25, 1.75)
    gate_matrix = gaussian(keys[8], (N_PIPE, D, EXPERTS * FFE), D ** -0.5, 0.09375, ((0, 8), (2, 32)))
    up_matrix = gaussian(keys[9], (N_PIPE, D, EXPERTS * FFE), D ** -0.5, 0.09375, ((0, 8), (2, 32)))
    down_matrix = gaussian(keys[10], (N_PIPE, EXPERTS * FFE, D), FFE ** -0.5, 0.1875, ((0, 8), (1, 32)))
    return {"forward_in": forward_in, "forward_route": forward_route, "forward_share": forward_share, "backward_in": backward_in, "backward_grad": backward_grad, "backward_route": backward_route, "backward_share": backward_share, "norm_gain": norm_gain, "gate_matrix": gate_matrix, "up_matrix": up_matrix, "down_matrix": down_matrix}


def normalize(values, gain_row):
    floats = values.astype(jnp.float32)
    scale_row = lax.rsqrt(lax.optimization_barrier(jnp.mean(floats * floats, axis=-1, keepdims=True)) + 1e-06)
    return (floats * scale_row * gain_row).astype(jnp.bfloat16)

def norm_backward(values, gain_row, d_normed):
    floats = values.astype(jnp.float32)
    scale_row = lax.rsqrt(lax.optimization_barrier(jnp.mean(floats * floats, axis=-1, keepdims=True)) + 1e-06)
    weighted = gain_row * d_normed
    return scale_row * weighted - floats * scale_row ** 3 * lax.optimization_barrier(jnp.mean(floats * weighted, axis=-1, keepdims=True))

def slot_rows(route_rows):
    blocks = route_rows.reshape(N_EXPERT, TOK_DEV * TOPK)
    onehot = (blocks[:, :, None] == jnp.arange(EXPERTS, dtype=jnp.int32)[None, None, :]).astype(jnp.int32)
    rank_in_expert = lax.optimization_barrier(jnp.sum((jnp.cumsum(onehot, axis=1) - 1) * onehot, axis=2))
    source = jnp.arange(N_EXPERT, dtype=jnp.int32)[:, None]
    flat_index = blocks * (N_EXPERT * CAP) + source * CAP + rank_in_expert
    return flat_index.reshape(-1).astype(jnp.int32)

def pack_rows(values, flat_index):
    empty = jnp.zeros((EXPERTS * N_EXPERT * CAP, values.shape[1]), values.dtype)
    return empty.at[flat_index].set(values)

def split_weights(gate_matrix, up_matrix, down_matrix):
    gate_blocks = gate_matrix.reshape(D, EXPERTS, FFE).transpose(1, 0, 2)
    up_blocks = up_matrix.reshape(D, EXPERTS, FFE).transpose(1, 0, 2)
    down_blocks = down_matrix.reshape(EXPERTS, FFE, D)
    return (gate_blocks, up_blocks, down_blocks)

def rounded_sum(running_sum, slice_part):
    return running_sum + lax.optimization_barrier(slice_part.astype(jnp.bfloat16)).astype(jnp.float32)

def expert_forward(packed, gate_matrix, up_matrix, down_matrix):
    gate_blocks, up_blocks, down_blocks = split_weights(gate_matrix, up_matrix, down_matrix)
    expert_rows = packed.reshape(EXPERTS, N_EXPERT * CAP, D)

    def one_expert(operands):
        rows_here, gate_block, up_block, down_block = operands
        pre_gate = jnp.dot(rows_here, gate_block, preferred_element_type=jnp.float32)
        pre_up = jnp.dot(rows_here, up_block, preferred_element_type=jnp.float32)
        hidden = (jax.nn.silu(pre_gate) * pre_up).astype(jnp.bfloat16)
        running_sum = jnp.zeros((N_EXPERT * CAP, D), jnp.float32)
        for slice_index in range(SLICES):
            low_edge = slice_index * H_DEV
            high_edge = low_edge + H_DEV
            slice_part = jnp.dot(hidden[:, low_edge:high_edge], down_block[low_edge:high_edge], preferred_element_type=jnp.float32)
            running_sum = rounded_sum(running_sum, slice_part)
        return lax.optimization_barrier(running_sum.astype(jnp.bfloat16))
    return lax.map(one_expert, (expert_rows, gate_blocks, up_blocks, down_blocks)).reshape(-1, D)

def expert_backward(packed, packed_grad, gate_matrix, up_matrix, down_matrix):
    gate_blocks, up_blocks, down_blocks = split_weights(gate_matrix, up_matrix, down_matrix)
    expert_rows = packed.reshape(EXPERTS, N_EXPERT * CAP, D)
    expert_grads = packed_grad.reshape(EXPERTS, N_EXPERT * CAP, D)
    contract = (((1,), (1,)), ((), ()))

    def one_expert(operands):
        rows_here, grads_here, gate_block, up_block, down_block = operands
        pre_gate = jnp.dot(rows_here, gate_block, preferred_element_type=jnp.float32)
        pre_up = jnp.dot(rows_here, up_block, preferred_element_type=jnp.float32)
        sigmoid_gate = jax.nn.sigmoid(pre_gate)
        d_hidden = lax.dot_general(grads_here, down_block, contract, preferred_element_type=jnp.float32)
        d_gate = (d_hidden * pre_up * sigmoid_gate * (1.0 + pre_gate * (1.0 - sigmoid_gate))).astype(jnp.bfloat16)
        d_up = (d_hidden * pre_gate * sigmoid_gate).astype(jnp.bfloat16)
        running_sum = jnp.zeros((N_EXPERT * CAP, D), jnp.float32)
        for slice_index in range(SLICES):
            low_edge = slice_index * H_DEV
            high_edge = low_edge + H_DEV
            slice_part = lax.dot_general(d_gate[:, low_edge:high_edge], gate_block[:, low_edge:high_edge], contract, preferred_element_type=jnp.float32)
            slice_part = slice_part + lax.dot_general(d_up[:, low_edge:high_edge], up_block[:, low_edge:high_edge], contract, preferred_element_type=jnp.float32)
            running_sum = rounded_sum(running_sum, slice_part)
        return lax.optimization_barrier(running_sum.astype(jnp.bfloat16))
    return lax.map(one_expert, (expert_rows, expert_grads, gate_blocks, up_blocks, down_blocks)).reshape(-1, D)

def reference(forward_in, forward_route, forward_share, backward_in, backward_grad, backward_route, backward_share, norm_gain, gate_matrix, up_matrix, down_matrix):
    forward_list = []
    backward_list = []
    for section_index in range(N_PIPE):
        section_input = forward_in[section_index]
        flat_index = slot_rows(forward_route[section_index])
        normed = normalize(section_input, norm_gain[section_index])
        packed = pack_rows(jnp.repeat(normed, TOPK, axis=0), flat_index)
        expert_out = expert_forward(packed, gate_matrix[section_index], up_matrix[section_index], down_matrix[section_index])
        picked = expert_out[flat_index].astype(jnp.float32).reshape(TOKENS, TOPK, D)
        mixed_rows = section_input.astype(jnp.float32) + lax.optimization_barrier(jnp.sum(forward_share[section_index][:, :, None] * picked, axis=1))
        forward_list.append(mixed_rows.astype(jnp.bfloat16))
        saved_input = backward_in[section_index]
        back_index = slot_rows(backward_route[section_index])
        normed_back = normalize(saved_input, norm_gain[section_index])
        section_grad = backward_grad[section_index]
        scaled = (backward_share[section_index][:, :, None] * section_grad.astype(jnp.float32)[:, None, :]).astype(jnp.bfloat16)
        packed_back = pack_rows(jnp.repeat(normed_back, TOPK, axis=0), back_index)
        packed_grad = pack_rows(scaled.reshape(-1, D), back_index)
        d_out = expert_backward(packed_back, packed_grad, gate_matrix[section_index], up_matrix[section_index], down_matrix[section_index])
        d_normed = lax.optimization_barrier(jnp.sum(d_out[back_index].astype(jnp.float32).reshape(TOKENS, TOPK, D), axis=1))
        d_input = section_grad.astype(jnp.float32) + norm_backward(saved_input, norm_gain[section_index], d_normed)
        backward_list.append(d_input.astype(jnp.bfloat16))
    next_forward = jnp.roll(jnp.stack(forward_list), 1, axis=0)
    next_backward = jnp.roll(jnp.stack(backward_list), -1, axis=0)
    return (next_forward, next_backward)
```

```python
import jax
import jax.numpy as jnp
from jax import lax
from jax.experimental import pallas as pl
from jax.experimental.pallas import tpu as pltpu
from jax.sharding import PartitionSpec as P

MESH = pl.DeviceIdType.MESH
NP, NZ, NY = 8, 8, 4
T = 128
D = 3584
C = 896
W = D + C
H = 256
KC = 512
NK = D // KC
F32, BF16 = jnp.float32, jnp.bfloat16
ORDER = (4, 3, 5, 2, 6, 1, 7)
NEAR = (1, 7, 2, 6, 3, 5, 4)


def dot_nn(a, b):
    return lax.dot_general(a, b, (((1,), (0,)), ((), ())), preferred_element_type=F32)


def dot_nt(a, b):
    return lax.dot_general(a, b, (((1,), (1,)), ((), ())), preferred_element_type=F32)


def iota(shape, dim):
    return lax.broadcasted_iota(jnp.int32, shape, dim)


def slots_of(route_row):
    onehot = (iota((16, T), 0) == route_row).astype(F32)
    before = (iota((T, T), 0) < iota((T, T), 1)).astype(F32).astype(BF16)
    count = dot_nn(onehot.astype(BF16), before)
    rank = jnp.sum(count * onehot, axis=0, keepdims=True)
    base = route_row.astype(F32) * 16.0
    main = jnp.where(rank < 15.5, base + rank, -1000.0)
    extra = jnp.where(rank < 15.5, -1000.0, base + rank - 16.0)
    return main, extra


def placing(slot_row):
    return (iota((T, T), 0).astype(F32) == slot_row).astype(F32)


def column(row):
    return jnp.transpose(jnp.broadcast_to(row, (T, T)))[:, 0:1]


def unfold(k):
    m, n = iota((32, T), 0), iota((32, T), 1)
    return (n == (m >> 2) * 16 + (m & 3) + 4 * k).astype(F32).astype(BF16)


def fold(k):
    n, m = iota((T, 32), 0), iota((T, 32), 1)
    return (n == (m >> 2) * 16 + (m & 3) + 4 * k).astype(F32).astype(BF16)


def kernel(
    fin, froute, fshare, bin_, bgrad, broute, bshare, gain, gate, up, down,
    nf, nb,
    xin, shp, meta_s, meta_r, gain_s, gain_r, send, recv, pair, extra,
    gate_o, up_o, down_o, gate_r, up_r, down_r,
    acc, hid, part_s, part_r, own, eo_b, eo_f, ret_s, ret_r, qbuf,
    lsem, zs, zr, ys, yr, ws, wr, ps, pr, rs, rr, xs, xr,
):
    p = lax.axis_index("pipe")
    i = lax.axis_index("expert")
    z, y = i // NY, i % NY
    core = p % 2
    nxt, prv = (p + 1) % NP, (p + NP - 1) % NP
    ya = y + 1 - 2 * (y % 2)
    yb = (y + NY - 1 + 2 * (y % 2)) % NY
    yt = ya * (1 - core) + yb * core
    yw = ya * core + yb * (1 - core)

    def at_z(pp, zz):
        return (pp, zz * NY + y)

    tok = (p, z * NY + yt)
    wgt = (p, z * NY + yw)

    def remote(src, dst, s, r, device):
        return pltpu.make_async_remote_copy(
            src_ref=src, dst_ref=dst, send_sem=s, recv_sem=r, device_id=device, device_id_type=MESH
        )

    bar = pltpu.get_barrier_semaphore()

    def greet(d, _):
        pl.semaphore_signal(bar, inc=1, device_id=at_z(nxt, (z + d) % NZ), device_id_type=MESH)
        pl.semaphore_signal(bar, inc=1, device_id=at_z(prv, (z + d) % NZ), device_id_type=MESH)
        return 0

    def greet_own(d, _):
        pl.semaphore_signal(bar, inc=1, device_id=at_z(p, (z + d) % NZ), device_id_type=MESH)
        return 0

    lax.fori_loop(0, NZ, greet, 0)
    lax.fori_loop(1, NZ, greet_own, 0)
    pl.semaphore_signal(bar, inc=1, device_id=tok, device_id_type=MESH)
    pl.semaphore_signal(bar, inc=1, device_id=wgt, device_id_type=MESH)

    loads = [
        pltpu.make_async_copy(bgrad.at[0], xin.at[0], lsem.at[0]),
        pltpu.make_async_copy(bin_.at[0], xin.at[1], lsem.at[1]),
        pltpu.make_async_copy(fin.at[0], xin.at[2], lsem.at[2]),
        pltpu.make_async_copy(down.at[0], down_o, lsem.at[3]),
        pltpu.make_async_copy(gate.at[0], gate_o, lsem.at[4]),
        pltpu.make_async_copy(up.at[0], up_o, lsem.at[5]),
    ]
    for c in loads:
        c.start()

    def pack(j, main, ex, chunk):
        pm = placing(main).astype(BF16)
        folded = jnp.zeros((T, C), F32)
        for k in range(4):
            v = chunk(k)
            send[j, :, :, k * C:(k + 1) * C] = dot_nn(pm, v).astype(BF16).reshape(NZ, 16, C)
            folded = folded + dot_nn(placing(ex + 4.0 * k).astype(BF16), v)
        send[j, :, :, D:] = folded.astype(BF16).reshape(NZ, 16, C)

    def inv_rms(ref):
        total = jnp.zeros((T, 1), F32)
        for k in range(4):
            v = ref[:, k * C:(k + 1) * C].astype(F32)
            total = total + jnp.sum(v * v, axis=1, keepdims=True)
        return lax.rsqrt(total / D + 1e-6)

    def z_copy(j, d):
        return remote(send.at[j, (z + d) % NZ], recv.at[j, z], zs.at[j, d], zr.at[j, d], at_z(p, (z + d) % NZ))

    def z_send(j):
        for d in ORDER:
            z_copy(j, d).start()

    def relay_copy(j, d):
        src = (z - d + NZ) % NZ
        ref = send.at[j, src] if d == 0 else recv.at[j, src]
        return remote(ref, pair.at[j, src], ys.at[j, d], yr.at[j, d], tok)

    def relay(j, ds):
        for d in ds:
            if d:
                z_copy(j, d).wait_recv()
            relay_copy(j, d).start()

    def keep(j):
        return pltpu.make_async_copy(send.at[j, z], recv.at[j, z], lsem.at[6 + j])

    bmain, bextra = slots_of(broute[...])
    loads[0].wait()
    share_col = column(bshare[...])
    pack(0, bmain, bextra, lambda k: (share_col * xin[0, :, k * C:(k + 1) * C].astype(F32)).astype(BF16))
    pl.semaphore_wait(bar, 25)
    z_send(0)
    weight_copies = [
        remote(down.at[0], down_r, ws.at[0], wr.at[0], wgt),
        remote(gate.at[0], gate_r, ws.at[1], wr.at[1], wgt),
        remote(up.at[0], up_r, ws.at[2], wr.at[2], wgt),
    ]
    weight_copies[0].start()
    relay(0, (0,))
    keep(0).start()
    weight_copies[1].start()
    weight_copies[2].start()

    loads[1].wait()
    r_back = inv_rms(xin.at[1])
    pack(1, bmain, bextra, lambda k: (
        xin[1, :, k * C:(k + 1) * C].astype(F32) * r_back * gain[:, k * C:(k + 1) * C]).astype(BF16))
    z_send(1)
    relay(1, (0,))
    keep(1).start()

    fmain, fextra = slots_of(froute[...])
    loads[2].wait()
    r_fwd = inv_rms(xin.at[2])
    pack(2, fmain, fextra, lambda k: (
        xin[2, :, k * C:(k + 1) * C].astype(F32) * r_fwd * gain[:, k * C:(k + 1) * C]).astype(BF16))

    def rows(*parts):
        return jnp.concatenate(list(parts) + [jnp.zeros((8 - len(parts), T), F32)], axis=0)

    meta_s[0] = rows(bmain, bextra)
    meta_s[1] = rows(fmain, fextra, fshare[...])
    gain_s[...] = jnp.broadcast_to(gain[...], (8, D))
    down_pipe, up_pipe = (prv, i), (nxt, i)
    ship = [
        remote(meta_s.at[0], meta_r.at[0], xs.at[0], xr.at[0], down_pipe),
        remote(gain_s, gain_r, xs.at[1], xr.at[1], down_pipe),
        remote(xin.at[0], shp.at[0], xs.at[2], xr.at[2], down_pipe),
        remote(xin.at[1], shp.at[1], xs.at[3], xr.at[3], down_pipe),
        remote(meta_s.at[1], meta_r.at[1], xs.at[4], xr.at[4], up_pipe),
        remote(xin.at[2], shp.at[2], xs.at[5], xr.at[5], up_pipe),
    ]
    for c in ship:
        c.start()

    relay(0, NEAR)
    z_send(2)
    relay(2, (0,))
    keep(2).start()

    def gather_extra(j):
        for k in range(4):
            u = unfold(k)
            extra[j, 0:32, k * C:(k + 1) * C] = dot_nn(u, pair[j, :, :, D:].reshape(T, C)).astype(BF16)
            extra[j, 32:64, k * C:(k + 1) * C] = dot_nn(u, recv[j, :, :, D:].reshape(T, C)).astype(BF16)

    def all_rows(j, ds):
        return jnp.concatenate([
            pair[j, :, :, ds].reshape(T, KC), extra[j, 0:32, ds],
            recv[j, :, :, ds].reshape(T, KC), extra[j, 32:64, ds]], axis=0)

    def first(j, mats):
        for m, _, _ in mats:
            acc[m] = jnp.zeros((320, H), F32)

        def step(n, _):
            ds = pl.ds(pl.multiple_of(n * KC, KC), KC)
            v = all_rows(j, ds)
            for m, w, transposed in mats:
                acc[m] += dot_nt(v, w[:, ds]) if transposed else dot_nn(v, w[ds, :])
            return 0

        lax.fori_loop(0, NK, step, 0)

    def arrived(j):
        keep(j).wait()
        for d in range(NZ):
            relay_copy(j, d).wait_recv()
        gather_extra(j)

    def part_copy(b, n):
        if isinstance(n, int) and n == NK:
            ds = pl.ds(D, C)
        else:
            ds = pl.ds(pl.multiple_of(n * KC, KC), KC)
        return remote(part_s.at[b, :, :, ds], part_r.at[b, :, :, ds], ps.at[b, n], pr.at[b, n], tok)

    def second(b, out):
        def theirs(n, _):
            ds = pl.ds(pl.multiple_of(n * KC, KC), KC)
            o = out(slice(0, 160), ds).astype(BF16)
            part_s[b, :, :, ds] = o[:T].reshape(NZ, 16, KC)
            eo_b[:, ds] = o[T:]
            part_copy(b, n).start()
            return 0

        lax.fori_loop(0, NK, theirs, 0)

        def fold_extra(dst):
            folded = jnp.zeros((T, C), F32)
            for k in range(4):
                folded = folded + dot_nn(fold(k), eo_b[:, k * C:(k + 1) * C])
            dst[b, :, :, D:] = folded.astype(BF16).reshape(NZ, 16, C)

        fold_extra(part_s)
        part_copy(b, NK).start()

        def ours(n, _):
            ds = pl.ds(pl.multiple_of(n * KC, KC), KC)
            o = out(slice(160, 320), ds)
            own[:, ds] = o[:T]
            eo_f[:, ds] = o[T:]
            return 0

        lax.fori_loop(0, NK, ours, 0)

        def add(n, _):
            ds = pl.ds(pl.multiple_of(n * KC, KC), KC)
            part_copy(b, n).wait_recv()
            o = own[:, ds] + part_r[b, :, :, ds].reshape(T, KC).astype(F32)
            ret_s[b, :, :, ds] = o.astype(BF16).reshape(NZ, 16, KC)
            return 0

        lax.fori_loop(0, NK, add, 0)
        part_copy(b, NK).wait_recv()
        for k in range(4):
            ks = slice(k * C, (k + 1) * C)
            theirs_k = dot_nn(unfold(k), part_r[b, :, :, D:].reshape(T, C))
            eo_b[:, ks] = (eo_f[:, ks] + theirs_k).astype(BF16)
        fold_extra(ret_s)

    def ret_copy(b, d):
        zz = (z + d) % NZ
        return remote(ret_s.at[b, zz], ret_r.at[b, z], rs.at[b, d], rr.at[b, d], at_z(prv if b == 0 else nxt, zz))

    loads[3].wait()
    arrived(0)
    weight_copies[0].wait_recv()
    first(0, [(0, down_o, True), (1, down_r, True)])
    relay(1, NEAR)
    loads[4].wait()
    loads[5].wait()
    arrived(1)
    weight_copies[1].wait_recv()
    weight_copies[2].wait_recv()
    first(1, [(2, gate_o, False), (3, gate_r, False), (4, up_o, False), (5, up_r, False)])

    def act_back(n, _):
        ds = pl.ds(pl.multiple_of(n * 32, 32), 32)
        for s in range(2):
            dh, pg, pu = acc[s, ds], acc[2 + s, ds], acc[4 + s, ds]
            sg = jax.nn.sigmoid(pg)
            hid[s, ds] = (dh * pu * sg * (1.0 + pg * (1.0 - sg))).astype(BF16)
            hid[2 + s, ds] = (dh * pg * sg).astype(BF16)
        return 0

    lax.fori_loop(0, 10, act_back, 0)

    def out_back(rows_, ds):
        return (dot_nt(hid[0, rows_], gate_o[ds, :]) + dot_nt(hid[1, rows_], gate_r[ds, :])
                + dot_nt(hid[2, rows_], up_o[ds, :]) + dot_nt(hid[3, rows_], up_r[ds, :]))

    second(0, out_back)
    for d in (4, 3, 5, 2, 6, 1, 7, 0):
        ret_copy(0, d).start()

    relay(2, NEAR)
    arrived(2)
    first(2, [(2, gate_o, False), (3, gate_r, False), (4, up_o, False), (5, up_r, False)])

    def act_fwd(n, _):
        ds = pl.ds(pl.multiple_of(n * 32, 32), 32)
        for s in range(2):
            pg, pu = acc[2 + s, ds], acc[4 + s, ds]
            hid[s, ds] = (pg * jax.nn.sigmoid(pg) * pu).astype(BF16)
        return 0

    lax.fori_loop(0, 10, act_fwd, 0)

    def out_fwd(rows_, ds):
        return dot_nn(hid[0, rows_], down_o[:, ds]) + dot_nn(hid[1, rows_], down_r[:, ds])

    second(1, out_fwd)
    for d in (4, 3, 5, 2, 6, 1, 7, 0):
        ret_copy(1, d).start()

    for c in ship:
        c.wait()

    def take(b, main, ex, k):
        g = jnp.transpose(placing(main)).astype(BF16)
        ge = jnp.transpose(placing(ex + 4.0 * k)).astype(BF16)
        return (dot_nn(g, ret_r[b, :, :, k * C:(k + 1) * C].reshape(T, C))
                + dot_nn(ge, ret_r[b, :, :, D:].reshape(T, C)))

    for d in range(NZ):
        ret_copy(0, d).wait_recv()
    main, ex = meta_r[0, 0:1, :], meta_r[0, 1:2, :]
    r = inv_rms(shp.at[1])
    total = jnp.zeros((T, 1), F32)
    for k in range(4):
        ks = slice(k * C, (k + 1) * C)
        q = gain_r[0:1, ks] * take(0, main, ex, k)
        qbuf[:, ks] = q
        total = total + jnp.sum(shp[1, :, ks].astype(F32) * q, axis=1, keepdims=True)
    coef = r * r * r * (total / D)
    for k in range(4):
        ks = slice(k * C, (k + 1) * C)
        nb[0, :, ks] = (shp[0, :, ks].astype(F32) + (r * qbuf[:, ks] - shp[1, :, ks].astype(F32) * coef)).astype(BF16)

    for d in range(NZ):
        ret_copy(1, d).wait_recv()
    main, ex = meta_r[1, 0:1, :], meta_r[1, 1:2, :]
    share_fwd = column(meta_r[1, 2:3, :])
    for k in range(4):
        ks = slice(k * C, (k + 1) * C)
        nf[0, :, ks] = (shp[2, :, ks].astype(F32) + share_fwd * take(1, main, ex, k)).astype(BF16)

    for j in range(3):
        for d in range(NZ):
            if d:
                z_copy(j, d).wait_send()
            relay_copy(j, d).wait_send()
        weight_copies[j].wait_send()
    for b in range(2):
        for n in range(NK + 1):
            part_copy(b, n).wait_send()
        for d in range(NZ):
            ret_copy(b, d).wait_send()


def per_device(fin, froute, fshare, bin_, bgrad, broute, bshare, gain, gate, up, down):
    vm = pl.BlockSpec(memory_space=pltpu.VMEM)
    hbm = pl.BlockSpec(memory_space=pl.ANY)
    dma = pltpu.SemaphoreType.DMA
    out = jax.ShapeDtypeStruct((1, T, D), BF16)
    v = pltpu.VMEM
    return pl.pallas_call(
        kernel,
        out_shape=(out, out),
        in_specs=[hbm, vm, vm, hbm, hbm, vm, vm, vm, hbm, hbm, hbm],
        out_specs=(vm, vm),
        scratch_shapes=[
            v((3, T, D), BF16), v((3, T, D), BF16), v((2, 8, T), F32), v((2, 8, T), F32),
            v((8, D), F32), v((8, D), F32),
            v((3, NZ, 16, W), BF16), v((3, NZ, 16, W), BF16), v((3, NZ, 16, W), BF16), v((3, 64, D), BF16),
            v((D, H), BF16), v((D, H), BF16), v((H, D), BF16),
            v((D, H), BF16), v((D, H), BF16), v((H, D), BF16),
            v((6, 320, H), F32), v((4, 320, H), BF16),
            v((2, NZ, 16, W), BF16), v((2, NZ, 16, W), BF16),
            v((T, D), F32), v((32, D), BF16), v((32, D), F32),
            v((2, NZ, 16, W), BF16), v((2, NZ, 16, W), BF16), v((T, D), F32),
            dma((9,)), dma((3, NZ)), dma((3, NZ)), dma((3, NZ)), dma((3, NZ)),
            dma((3,)), dma((3,)), dma((2, NK + 1)), dma((2, NK + 1)),
            dma((2, NZ)), dma((2, NZ)), dma((6,)), dma((6,)),
        ],
        compiler_params=pltpu.CompilerParams(
            collective_id=1, has_side_effects=True, vmem_limit_bytes=60 << 20
        ),
        name="dualpipe_step",
    )(
        fin, froute.reshape(1, T), fshare.reshape(1, T), bin_, bgrad, broute.reshape(1, T),
        bshare.reshape(1, T), gain, gate, up, down,
    )


def solution(mesh):
    spec = P("pipe", "expert", None)
    return jax.shard_map(
        per_device,
        mesh=mesh,
        in_specs=(
            spec, spec, spec, spec, spec, spec, spec,
            P("pipe", None), P("pipe", None, "expert"), P("pipe", None, "expert"), P("pipe", "expert", None),
        ),
        out_specs=(spec, spec),
        check_vma=False,
    )
```

```python
import jax
import jax.numpy as jnp
from jax import lax
from jax.experimental import pallas as pl
from jax.experimental.pallas import tpu as pltpu
from jax.sharding import PartitionSpec as P

MESH = pl.DeviceIdType.MESH
NP, NZ, NY = 8, 8, 4
T = 128
D = 3584
C = 896
W = D + C
H = 256
KC = 512
NK = D // KC
F32, BF16 = jnp.float32, jnp.bfloat16
ORDER = (4, 3, 5, 2, 6, 1, 7)
NEAR = (1, 7, 2, 6, 3, 5, 4)
FAR = (4, 3, 5, 2, 6, 1, 7, 0)
GROUPS = ((0, 2048), (2048, 2432))
LAG = 3
HALF0, HALF1, ALL = (0, 4), (4, 4), (0, 8)


def dot_nn(a, b):
    return lax.dot_general(a, b, (((1,), (0,)), ((), ())), preferred_element_type=F32)


def dot_nt(a, b):
    return lax.dot_general(a, b, (((1,), (1,)), ((), ())), preferred_element_type=F32)


def iota(shape, dim):
    return lax.broadcasted_iota(jnp.int32, shape, dim)


def slots_of(route_row, z):
    onehot = (iota((16, T), 0) == route_row).astype(F32)
    before = (iota((T, T), 0) < iota((T, T), 1)).astype(F32).astype(BF16)
    count = dot_nn(onehot.astype(BF16), before)
    rank = jnp.sum(count * onehot, axis=0, keepdims=True)
    place = jnp.zeros_like(rank)
    for n, d in enumerate(FAR):
        place = place + jnp.where(route_row == (z + d) % NZ, float(n), 0.0)
    slots = []
    for base in (route_row.astype(F32) * 16.0, place * 16.0):
        slots.append(jnp.where(rank < 15.5, base + rank, -1000.0))
        slots.append(jnp.where(rank < 15.5, -1000.0, base + rank - 16.0))
    return slots


def placing(slot_row):
    return (iota((T, T), 0).astype(F32) == slot_row).astype(F32)


def column(row):
    return jnp.transpose(jnp.broadcast_to(row, (T, T)))[:, 0:1]


def unfold(k, nb):
    m, n = iota((4 * nb, 16 * nb), 0), iota((4 * nb, 16 * nb), 1)
    return (n == (m >> 2) * 16 + (m & 3) + 4 * k).astype(F32).astype(BF16)


def fold(k, nb):
    n, m = iota((16 * nb, 4 * nb), 0), iota((16 * nb, 4 * nb), 1)
    return (n == (m >> 2) * 16 + (m & 3) + 4 * k).astype(F32).astype(BF16)


def kernel(
    fin, froute, fshare, bin_, bgrad, broute, bshare, gain, gate, up, down,
    nf, nb,
    xin, shp, meta_s, meta_r, gain_s, gain_r, send, recv, pair, extra,
    gate_o, up_o, down_o, gate_r, up_r, down_r,
    acc, hid, part_s, part_r, own, eo_b, eo_f, ret_s, ret_r, qbuf, pick, outs,
    lsem, zs, zr, ys, yr, ws, wr, ps, pr, rs, rr, xs, xr, osem,
):
    p = lax.axis_index("pipe")
    i = lax.axis_index("expert")
    z, y = i // NY, i % NY
    core = p % 2
    nxt, prv = (p + 1) % NP, (p + NP - 1) % NP
    ya = y + 1 - 2 * (y % 2)
    yb = (y + NY - 1 + 2 * (y % 2)) % NY
    yt = ya * (1 - core) + yb * core
    yw = ya * core + yb * (1 - core)

    def at_z(pp, zz):
        return (pp, zz * NY + y)

    tok = (p, z * NY + yt)
    wgt = (p, z * NY + yw)

    def remote(src, dst, s, r, device):
        return pltpu.make_async_remote_copy(
            src_ref=src, dst_ref=dst, send_sem=s, recv_sem=r, device_id=device, device_id_type=MESH
        )

    bar = pltpu.get_barrier_semaphore()

    def greet(d, _):
        pl.semaphore_signal(bar, inc=1, device_id=at_z(nxt, (z + d) % NZ), device_id_type=MESH)
        pl.semaphore_signal(bar, inc=1, device_id=at_z(prv, (z + d) % NZ), device_id_type=MESH)
        return 0

    def greet_own(d, _):
        pl.semaphore_signal(bar, inc=1, device_id=at_z(p, (z + d) % NZ), device_id_type=MESH)
        return 0

    lax.fori_loop(0, NZ, greet, 0)
    lax.fori_loop(1, NZ, greet_own, 0)
    pl.semaphore_signal(bar, inc=1, device_id=tok, device_id_type=MESH)
    pl.semaphore_signal(bar, inc=1, device_id=wgt, device_id_type=MESH)

    loads = [
        pltpu.make_async_copy(bgrad.at[0], xin.at[0], lsem.at[0]),
        pltpu.make_async_copy(bin_.at[0], xin.at[1], lsem.at[1]),
        pltpu.make_async_copy(fin.at[0], xin.at[2], lsem.at[2]),
        pltpu.make_async_copy(down.at[0], down_o, lsem.at[3]),
        pltpu.make_async_copy(gate.at[0], gate_o, lsem.at[4]),
        pltpu.make_async_copy(up.at[0], up_o, lsem.at[5]),
    ]
    for n in (2, 0, 1, 4, 5, 3):
        loads[n].start()

    def pack(j, main, ex, chunk):
        pm = placing(main).astype(BF16)
        folded = jnp.zeros((T, C), F32)
        for k in range(4):
            v = chunk(k)
            send[j, :, :, k * C:(k + 1) * C] = dot_nn(pm, v).astype(BF16).reshape(NZ, 16, C)
            folded = folded + dot_nn(placing(ex + 4.0 * k).astype(BF16), v)
        send[j, :, :, D:] = folded.astype(BF16).reshape(NZ, 16, C)

    def inv_rms(ref):
        total = jnp.zeros((T, 1), F32)
        for k in range(4):
            v = ref[:, k * C:(k + 1) * C].astype(F32)
            total = total + jnp.sum(v * v, axis=1, keepdims=True)
        return lax.rsqrt(total / D + 1e-6)

    def pack_normed(j, main, ex):
        loads[j].wait()
        r = inv_rms(xin.at[j])
        pack(j, main, ex, lambda k: (
            xin[j, :, k * C:(k + 1) * C].astype(F32) * r * gain[:, k * C:(k + 1) * C]).astype(BF16))

    def z_copy(j, d):
        return remote(send.at[j, (z + d) % NZ], recv.at[j, z], zs.at[j, d], zr.at[j, d], at_z(p, (z + d) % NZ))

    def relay_copy(j, d):
        src = (z - d + NZ) % NZ
        ref = send.at[j, src] if d == 0 else recv.at[j, src]
        return remote(ref, pair.at[j, src], ys.at[j, d], yr.at[j, d], tok)

    def relay(j, ds):
        for d in ds:
            if d:
                z_copy(j, d).wait_recv()
            relay_copy(j, d).start()

    def keep(j):
        return pltpu.make_async_copy(send.at[j, z], recv.at[j, z], lsem.at[6 + j])

    def z_send(j):
        for d in ORDER:
            z_copy(j, d).start()
        keep(j).start()

    weight_copies = [
        remote(gate.at[0], gate_r, ws.at[0], wr.at[0], wgt),
        remote(up.at[0], up_r, ws.at[1], wr.at[1], wgt),
        remote(down.at[0], down_r, ws.at[2], wr.at[2], wgt),
    ]

    fmain, fextra, ftake, ftake_ex = slots_of(froute[...], z)
    pack_normed(2, fmain, fextra)
    pl.semaphore_wait(bar, 25)
    for c in weight_copies:
        c.start()
    z_send(2)

    bmain, bextra, btake, btake_ex = slots_of(broute[...], z)
    loads[0].wait()
    share_col = column(bshare[...])
    pack(0, bmain, bextra, lambda k: (share_col * xin[0, :, k * C:(k + 1) * C].astype(F32)).astype(BF16))
    z_send(0)
    pack_normed(1, bmain, bextra)
    z_send(1)

    def rows(*parts):
        return jnp.concatenate(list(parts) + [jnp.zeros((8 - len(parts), T), F32)], axis=0)

    meta_s[0] = rows(btake, btake_ex)
    meta_s[1] = rows(ftake, ftake_ex, fshare[...])
    gain_s[...] = jnp.broadcast_to(gain[...], (8, D))
    down_pipe, up_pipe = (prv, i), (nxt, i)
    ship = [
        remote(meta_s.at[0], meta_r.at[0], xs.at[0], xr.at[0], down_pipe),
        remote(gain_s, gain_r, xs.at[1], xr.at[1], down_pipe),
        remote(xin.at[0], shp.at[0], xs.at[2], xr.at[2], down_pipe),
        remote(xin.at[1], shp.at[1], xs.at[3], xr.at[3], down_pipe),
        remote(meta_s.at[1], meta_r.at[1], xs.at[4], xr.at[4], up_pipe),
        remote(xin.at[2], shp.at[2], xs.at[5], xr.at[5], up_pipe),
    ]
    for c in ship:
        c.start()

    PAIR, OWN = 0, 160

    def source(n):
        return (z - FAR[n] + NZ) % NZ

    def first(j, part, half, mats):
        src = recv if part else pair
        pos, nb = half
        e0 = (32 if part else 0) + 4 * pos

        def blocks(ds):
            return [src[j, source(n), :, ds] for n in range(pos, pos + nb)]

        folded = jnp.concatenate(blocks(slice(D, W)), axis=0)
        for k in range(4):
            extra[j, e0:e0 + 4 * nb, k * C:(k + 1) * C] = dot_nn(unfold(k, nb), folded).astype(BF16)
        at = pl.ds(part + 16 * pos, 16 * nb)
        at_ex = pl.ds(part + 128 + 4 * pos, 4 * nb)
        for m, _, _ in mats:
            acc[m, at] = jnp.zeros((16 * nb, H), F32)
            acc[m, at_ex] = jnp.zeros((4 * nb, H), F32)

        def step(n, _):
            ds = pl.ds(pl.multiple_of(n * KC, KC), KC)
            v = jnp.concatenate(blocks(ds) + [extra[j, e0:e0 + 4 * nb, ds]], axis=0)
            for m, w, transposed in mats:
                o = dot_nt(v, w[:, ds]) if transposed else dot_nn(v, w[ds, :])
                acc[m, at] += o[:16 * nb]
                acc[m, at_ex] += o[16 * nb:]
            return 0

        lax.fori_loop(0, NK, step, 0)

    def have_pair(j, half):
        for n in range(half[0], half[0] + half[1]):
            relay_copy(j, FAR[n]).wait_recv()

    gate_up = [(2, gate_o, False), (3, gate_r, False), (4, up_o, False), (5, up_r, False)]
    downs = [(0, down_o, True), (1, down_r, True)]

    def act(fn, part, half):
        pos, nb = half

        def step(n, _):
            fn(pl.ds(pl.multiple_of(part + 16 * pos + n * 32, 32), 32))
            return 0

        lax.fori_loop(0, nb // 2, step, 0)
        fn(pl.ds(part + 128 + 4 * pos, 4 * nb))

    def act_fwd(ds):
        for s in range(2):
            pg, pu = acc[2 + s, ds], acc[4 + s, ds]
            hid[s, ds] = (pg * jax.nn.sigmoid(pg) * pu).astype(BF16)

    def act_back(ds):
        for s in range(2):
            dh, pg, pu = acc[s, ds], acc[2 + s, ds], acc[4 + s, ds]
            sg = jax.nn.sigmoid(pg)
            hid[2 + s, ds] = (dh * pu * sg * (1.0 + pg * (1.0 - sg))).astype(BF16)
            hid[4 + s, ds] = (dh * pg * sg).astype(BF16)

    def hidden(n, part, half):
        pos, nb = half
        return jnp.concatenate(
            [hid[n, pl.ds(part + 16 * pos, 16 * nb)], hid[n, pl.ds(part + 128 + 4 * pos, 4 * nb)]], axis=0)

    def out_rows(b, part, half, ds):
        h = [hidden(n, part, half) for n in ((2, 3, 4, 5) if b == 0 else (0, 1))]
        if b == 1:
            return dot_nn(h[0], down_o[:, ds]) + dot_nn(h[1], down_r[:, ds])
        return (dot_nt(h[0], gate_o[ds, :]) + dot_nt(h[1], gate_r[ds, :])
                + dot_nt(h[2], up_o[ds, :]) + dot_nt(h[3], up_r[ds, :]))

    def cols(n):
        return pl.ds(n * KC, KC) if isinstance(n, int) else pl.ds(pl.multiple_of(n * KC, KC), KC)

    def part_copy(b, half, n):
        ds = pl.ds(D, C) if isinstance(n, int) and n == NK else cols(n)
        at, h = pl.ds(*half), half[0] // 4
        return remote(part_s.at[b, at, :, ds], part_r.at[b, at, :, ds], ps.at[b, h, n], pr.at[b, h, n], tok)

    def fold_extra(dst, b, half):
        pos, nb = half
        folded = jnp.zeros((16 * nb, C), F32)
        for k in range(4):
            folded = folded + dot_nn(fold(k, nb), eo_b[4 * pos:4 * (pos + nb), k * C:(k + 1) * C])
        dst[b, pos:pos + nb, :, D:] = folded.astype(BF16).reshape(nb, 16, C)

    def theirs(b, half, n):
        pos, nb = half
        ds = cols(n)
        o = out_rows(b, PAIR, half, ds).astype(BF16)
        part_s[b, pos:pos + nb, :, ds] = o[:16 * nb].reshape(nb, 16, KC)
        eo_b[4 * pos:4 * (pos + nb), ds] = o[16 * nb:]
        part_copy(b, half, n).start()

    def theirs_extra(b, half):
        fold_extra(part_s, b, half)
        part_copy(b, half, NK).start()

    def ours(b, half, n):
        pos, nb = half
        ds = cols(n)
        o = out_rows(b, OWN, half, ds)
        own[16 * pos:16 * (pos + nb), ds] = o[:16 * nb]
        eo_f[4 * pos:4 * (pos + nb), ds] = o[16 * nb:]

    def ret_copy(b, g, n):
        ds = pl.ds(*GROUPS[g])
        return remote(ret_s.at[b, n, :, ds], ret_r.at[b, n, :, ds], rs.at[b, g, n], rr.at[b, g, n],
                      at_z(prv if b == 0 else nxt, source(n)))

    def ret_send(b, half, g):
        for n in range(half[0], half[0] + half[1]):
            ret_copy(b, g, n).start()

    def add(b, half, n):
        pos, nb = half
        ds = cols(n)
        part_copy(b, half, n).wait_recv()
        o = own[16 * pos:16 * (pos + nb), ds] + part_r[b, pos:pos + nb, :, ds].reshape(16 * nb, KC).astype(F32)
        ret_s[b, pos:pos + nb, :, ds] = o.astype(BF16).reshape(nb, 16, KC)
        if n == 3:
            ret_send(b, half, 0)

    def add_extra(b, half):
        pos, nb = half
        part_copy(b, half, NK).wait_recv()
        folded = part_r[b, pos:pos + nb, :, D:].reshape(16 * nb, C)
        for k in range(4):
            ks = slice(k * C, (k + 1) * C)
            at = slice(4 * pos, 4 * (pos + nb))
            eo_b[at, ks] = (eo_f[at, ks] + dot_nn(unfold(k, nb), folded)).astype(BF16)
        fold_extra(ret_s, b, half)
        ret_send(b, half, 1)

    def repeat(fn, b, half):
        def step(n, _):
            fn(b, half, n)
            return 0

        lax.fori_loop(0, NK, step, 0)

    def add_all(b, half):
        for n in range(NK):
            add(b, half, n)
        add_extra(b, half)

    def back_end(half):
        for n in range(NK + LAG):
            if n < NK:
                theirs(0, half, n)
            if n == NK - 1:
                theirs_extra(0, half)
            if n >= LAG:
                ours(0, half, n - LAG)
                add(0, half, n - LAG)
        add_extra(0, half)

    relay(2, (0,) + NEAR)
    keep(2).wait()
    loads[4].wait()
    loads[5].wait()
    loads[3].wait()
    weight_copies[0].wait_recv()
    weight_copies[1].wait_recv()
    first(2, OWN, ALL, gate_up)
    act(act_fwd, OWN, ALL)
    have_pair(2, ALL)
    first(2, PAIR, ALL, gate_up)
    act(act_fwd, PAIR, ALL)
    weight_copies[2].wait_recv()
    repeat(theirs, 1, ALL)
    theirs_extra(1, ALL)
    relay(0, FAR[:4])
    relay(1, FAR[:4])
    relay(0, FAR[4:])
    repeat(ours, 1, ALL)
    for d in NEAR:
        if d in FAR[4:]:
            z_copy(1, d).wait_recv()
    keep(0).wait()
    first(0, OWN, ALL, downs)
    keep(1).wait()
    first(1, OWN, ALL, gate_up)
    act(act_back, OWN, ALL)
    add_all(1, ALL)
    have_pair(0, HALF0)
    first(0, PAIR, HALF0, downs)
    have_pair(1, HALF0)
    first(1, PAIR, HALF0, gate_up)
    act(act_back, PAIR, HALF0)
    repeat(theirs, 0, HALF0)
    theirs_extra(0, HALF0)
    for d in FAR[4:]:
        relay_copy(1, d).start()
    repeat(ours, 0, HALF0)
    have_pair(0, HALF1)
    first(0, PAIR, HALF1, downs)
    add_all(0, HALF0)
    have_pair(1, HALF1)
    first(1, PAIR, HALF1, gate_up)
    act(act_back, PAIR, HALF1)
    back_end(HALF1)

    for c in ship:
        c.wait()
    for b in range(2):
        main, ex = meta_r[b, 0:1, :], meta_r[b, 1:2, :]
        pick[b, 0] = jnp.transpose(placing(main)).astype(BF16)
        for k in range(4):
            pick[b, 1 + k] = jnp.transpose(placing(ex + 4.0 * k)).astype(BF16)

    def take(b, half, k):
        pos, nb = half
        at = slice(16 * pos, 16 * (pos + nb))
        main = ret_r[b, pos:pos + nb, :, k * C:(k + 1) * C].reshape(16 * nb, C)
        return dot_nn(pick[b, 0][:, at], main) + dot_nn(
            pick[b, 1 + k][:, at], ret_r[b, pos:pos + nb, :, D:].reshape(16 * nb, C))

    def have_ret(b, half):
        for g in range(2):
            for n in range(half[0], half[0] + half[1]):
                ret_copy(b, g, n).wait_recv()

    share_fwd = column(meta_r[1, 2:3, :])
    r = inv_rms(shp.at[1])
    have_ret(1, ALL)
    for k in range(4):
        ks = slice(k * C, (k + 1) * C)
        outs[1, :, ks] = (shp[2, :, ks].astype(F32) + share_fwd * take(1, ALL, k)).astype(BF16)
    out_f = pltpu.make_async_copy(outs.at[1], nf.at[0], osem.at[0])
    out_f.start()

    have_ret(0, HALF0)
    for k in range(4):
        qbuf[:, k * C:(k + 1) * C] = take(0, HALF0, k)
    for j in range(3):
        for d in range(NZ):
            if d:
                z_copy(j, d).wait_send()
            relay_copy(j, d).wait_send()
        weight_copies[j].wait_send()
    for b, half in ((1, ALL), (0, HALF0), (0, HALF1)):
        for n in range(NK + 1):
            part_copy(b, half, n).wait_send()
    for b in range(2):
        for g in range(2):
            for n in range(NZ):
                ret_copy(b, g, n).wait_send()

    have_ret(0, HALF1)
    total = jnp.zeros((T, 1), F32)
    for k in range(4):
        ks = slice(k * C, (k + 1) * C)
        q = gain_r[0:1, ks] * (qbuf[:, ks] + take(0, HALF1, k))
        qbuf[:, ks] = q
        total = total + jnp.sum(shp[1, :, ks].astype(F32) * q, axis=1, keepdims=True)
    coef = r * r * r * (total / D)
    out_b = []
    for k in range(4):
        ks = slice(k * C, (k + 1) * C)
        outs[0, :, ks] = (
            shp[0, :, ks].astype(F32) + (r * qbuf[:, ks] - shp[1, :, ks].astype(F32) * coef)).astype(BF16)
        out_b.append(pltpu.make_async_copy(outs.at[0, :, pl.ds(k * C, C)], nb.at[0, :, pl.ds(k * C, C)], osem.at[1 + k]))
        out_b[-1].start()

    out_f.wait()
    for c in out_b:
        c.wait()


def per_device(fin, froute, fshare, bin_, bgrad, broute, bshare, gain, gate, up, down):
    vm = pl.BlockSpec(memory_space=pltpu.VMEM)
    hbm = pl.BlockSpec(memory_space=pl.ANY)
    dma = pltpu.SemaphoreType.DMA
    out = jax.ShapeDtypeStruct((1, T, D), BF16)
    v = pltpu.VMEM
    return pl.pallas_call(
        kernel,
        out_shape=(out, out),
        in_specs=[hbm, vm, vm, hbm, hbm, vm, vm, vm, hbm, hbm, hbm],
        out_specs=(hbm, hbm),
        scratch_shapes=[
            v((3, T, D), BF16), v((3, T, D), BF16), v((2, 8, T), F32), v((2, 8, T), F32),
            v((8, D), F32), v((8, D), F32),
            v((3, NZ, 16, W), BF16), v((3, NZ, 16, W), BF16), v((3, NZ, 16, W), BF16), v((3, 64, D), BF16),
            v((D, H), BF16), v((D, H), BF16), v((H, D), BF16),
            v((D, H), BF16), v((D, H), BF16), v((H, D), BF16),
            v((6, 320, H), F32), v((6, 320, H), BF16),
            v((2, NZ, 16, W), BF16), v((2, NZ, 16, W), BF16),
            v((T, D), F32), v((32, D), BF16), v((32, D), F32),
            v((2, NZ, 16, W), BF16), v((2, NZ, 16, W), BF16), v((T, D), F32),
            v((2, 5, T, T), BF16), v((2, T, D), BF16),
            dma((9,)), dma((3, NZ)), dma((3, NZ)), dma((3, NZ)), dma((3, NZ)),
            dma((3,)), dma((3,)), dma((2, 2, NK + 1)), dma((2, 2, NK + 1)),
            dma((2, 2, NZ)), dma((2, 2, NZ)), dma((6,)), dma((6,)), dma((5,)),
        ],
        compiler_params=pltpu.CompilerParams(
            collective_id=1, has_side_effects=True, vmem_limit_bytes=60 << 20
        ),
        name="dualpipe_step",
    )(
        fin, froute.reshape(1, T), fshare.reshape(1, T), bin_, bgrad, broute.reshape(1, T),
        bshare.reshape(1, T), gain, gate, up, down,
    )


def solution(mesh):
    spec = P("pipe", "expert", None)
    return jax.shard_map(
        per_device,
        mesh=mesh,
        in_specs=(
            spec, spec, spec, spec, spec, spec, spec,
            P("pipe", None), P("pipe", None, "expert"), P("pipe", None, "expert"), P("pipe", "expert", None),
        ),
        out_specs=(spec, spec),
        check_vma=False,
    )
```

```python
import jax
import jax.numpy as jnp
from jax import lax
from jax.experimental import pallas as pl
from jax.experimental.pallas import tpu as pltpu
from jax.sharding import PartitionSpec as P

MESH = pl.DeviceIdType.MESH
NP, NZ, NY = 8, 8, 4
T = 128
D = 3584
C = 896
W = D + C
H = 256
KC = 512
NK = D // KC
F32, BF16 = jnp.float32, jnp.bfloat16
ORDER = (4, 3, 5, 2, 6, 1, 7)
NEAR = (1, 7, 2, 6, 3, 5, 4)
FAR = (4, 3, 5, 2, 6, 1, 7, 0)
COLS = ((0, 1024), (1024, 1024), (2048, 1024), (3072, 1408))
GROUP = ((0, 3), (3, 3), (6, 2))
NG = len(GROUP)
ALL = tuple(range(NG))
PART = T + 16 * NG


def span(gs):
    return GROUP[gs[0]][0], sum(GROUP[g][1] for g in gs)


def dot_nn(a, b):
    return lax.dot_general(a, b, (((1,), (0,)), ((), ())), preferred_element_type=F32)


def dot_nt(a, b):
    return lax.dot_general(a, b, (((1,), (1,)), ((), ())), preferred_element_type=F32)


def iota(shape, dim):
    return lax.broadcasted_iota(jnp.int32, shape, dim)


def slots_of(route_row, z):
    onehot = (iota((16, T), 0) == route_row).astype(F32)
    before = (iota((T, T), 0) < iota((T, T), 1)).astype(F32).astype(BF16)
    count = dot_nn(onehot.astype(BF16), before)
    rank = jnp.sum(count * onehot, axis=0, keepdims=True)
    place = jnp.zeros_like(rank)
    for n, d in enumerate(FAR):
        place = place + jnp.where(route_row == (z + d) % NZ, float(n), 0.0)
    slots = []
    for base in (route_row.astype(F32) * 16.0, place * 16.0):
        slots.append(jnp.where(rank < 15.5, base + rank, -1000.0))
        slots.append(jnp.where(rank < 15.5, -1000.0, base + rank - 16.0))
    return slots


def placing(slot_row):
    return (iota((T, T), 0).astype(F32) == slot_row).astype(F32)


def column(row):
    return jnp.transpose(jnp.broadcast_to(row, (T, T)))[:, 0:1]


def unfold(k, nb):
    m, n = iota((16, 16 * nb), 0), iota((16, 16 * nb), 1)
    return (n == (m >> 2) * 16 + (m & 3) + 4 * k).astype(F32).astype(BF16)


def fold(k, nb):
    n, m = iota((16 * nb, 16), 0), iota((16 * nb, 16), 1)
    return (n == (m >> 2) * 16 + (m & 3) + 4 * k).astype(F32).astype(BF16)


def kernel(
    fin, froute, fshare, bin_, bgrad, broute, bshare, gain, gate, up, down,
    nf, nb,
    xin, shp, meta_s, meta_r, gain_s, gain_r, send, recv, pair, extra,
    gate_o, up_o, down_o, gate_r, up_r, down_r,
    acc, hid, part_s, part_r, own, eo_b, eo_f, ret_s, ret_r, qbuf, pick0, pick1, outs,
    lsem, zs, zr, zrf, ys, yr, ws, wr, ps, pr, rs, rr, xs, xr, osem,
):
    p = lax.axis_index("pipe")
    i = lax.axis_index("expert")
    z, y = i // NY, i % NY
    core = p % 2
    nxt, prv = (p + 1) % NP, (p + NP - 1) % NP
    ya = y + 1 - 2 * (y % 2)
    yb = (y + NY - 1 + 2 * (y % 2)) % NY
    yt = ya * (1 - core) + yb * core
    yw = ya * core + yb * (1 - core)

    def at_z(pp, zz):
        return (pp, zz * NY + y)

    tok = (p, z * NY + yt)
    wgt = (p, z * NY + yw)

    def remote(src, dst, s, r, device):
        return pltpu.make_async_remote_copy(
            src_ref=src, dst_ref=dst, send_sem=s, recv_sem=r, device_id=device, device_id_type=MESH
        )

    loads = [
        pltpu.make_async_copy(bgrad.at[0], xin.at[0], lsem.at[0]),
        pltpu.make_async_copy(bin_.at[0], xin.at[1], lsem.at[1]),
        pltpu.make_async_copy(fin.at[0], xin.at[2], lsem.at[2]),
        pltpu.make_async_copy(down.at[0], down_o, lsem.at[3]),
        pltpu.make_async_copy(gate.at[0], gate_o, lsem.at[4]),
        pltpu.make_async_copy(up.at[0], up_o, lsem.at[5]),
    ]
    for n in (2, 0, 1, 4, 5, 3):
        loads[n].start()

    bar = pltpu.get_barrier_semaphore()

    def greet(d, _):
        pl.semaphore_signal(bar, inc=1, device_id=at_z(nxt, (z + d) % NZ), device_id_type=MESH)
        pl.semaphore_signal(bar, inc=1, device_id=at_z(prv, (z + d) % NZ), device_id_type=MESH)
        return 0

    def greet_own(d, _):
        pl.semaphore_signal(bar, inc=1, device_id=at_z(p, (z + d) % NZ), device_id_type=MESH)
        return 0

    lax.fori_loop(0, NZ, greet, 0)
    lax.fori_loop(1, NZ, greet_own, 0)
    pl.semaphore_signal(bar, inc=1, device_id=tok, device_id_type=MESH)
    pl.semaphore_signal(bar, inc=1, device_id=wgt, device_id_type=MESH)

    def pack(j, main, ex, chunk):
        pm = placing(main).astype(BF16)
        folded = jnp.zeros((T, C), F32)
        for k in range(4):
            v = chunk(k)
            send[j, :, :, k * C:(k + 1) * C] = dot_nn(pm, v).astype(BF16).reshape(NZ, 16, C)
            folded = folded + dot_nn(placing(ex + 4.0 * k).astype(BF16), v)
        send[j, :, :, D:] = folded.astype(BF16).reshape(NZ, 16, C)

    def inv_rms(ref):
        total = jnp.zeros((T, 1), F32)
        for k in range(4):
            v = ref[:, k * C:(k + 1) * C].astype(F32)
            total = total + jnp.sum(v * v, axis=1, keepdims=True)
        return lax.rsqrt(total / D + 1e-6)

    def pack_normed(j, main, ex):
        loads[j].wait()
        r = inv_rms(xin.at[j])
        pack(j, main, ex, lambda k: (
            xin[j, :, k * C:(k + 1) * C].astype(F32) * r * gain[:, k * C:(k + 1) * C]).astype(BF16))

    def z_copy(j, d):
        return remote(send.at[j, (z + d) % NZ], recv.at[j, z], zs.at[j],
                      zrf.at[d] if j == 2 else zr.at[j], at_z(p, (z + d) % NZ))

    def z_all(j):
        return remote(send.at[j, pl.ds(0, 7)], recv.at[j, pl.ds(0, 7)], zs.at[j], zr.at[j % 2], tok)

    def relay_copy(j, d):
        src = (z - d + NZ) % NZ
        ref = send.at[j, src] if d == 0 else recv.at[j, src]
        g = 0
        if j < 2:
            g = [d in FAR[lo:lo + nb] for lo, nb in GROUP].index(True)
        return remote(ref, pair.at[j, src], ys.at[j], yr.at[j, g], tok)

    def relay_all(j, nb, g):
        return remote(recv.at[j, pl.ds(0, nb)], pair.at[j, pl.ds(0, nb)], ys.at[j], yr.at[j, g], tok)

    def relay(j, ds):
        for d in ds:
            relay_copy(j, d).start()

    def keep(j):
        return pltpu.make_async_copy(send.at[j, z], recv.at[j, z], lsem.at[6 + j])

    def z_send(j):
        for d in ORDER:
            z_copy(j, d).start()
        keep(j).start()

    weight_copies = [
        remote(gate.at[0], gate_r, ws.at[0], wr.at[0], wgt),
        remote(up.at[0], up_r, ws.at[1], wr.at[1], wgt),
        remote(down.at[0], down_r, ws.at[2], wr.at[2], wgt),
    ]

    pl.semaphore_wait(bar, 25)
    for c in weight_copies:
        c.start()
    fmain, fextra, ftake, ftake_ex = slots_of(froute[...], z)
    pack_normed(2, fmain, fextra)
    z_send(2)

    bmain, bextra, btake, btake_ex = slots_of(broute[...], z)
    loads[0].wait()
    share_col = column(bshare[...])
    pack(0, bmain, bextra, lambda k: (share_col * xin[0, :, k * C:(k + 1) * C].astype(F32)).astype(BF16))
    z_send(0)
    pack_normed(1, bmain, bextra)
    z_send(1)

    def rows(*parts):
        return jnp.concatenate(list(parts) + [jnp.zeros((8 - len(parts), T), F32)], axis=0)

    meta_s[0] = rows(btake, btake_ex)
    meta_s[1] = rows(ftake, ftake_ex, fshare[...])
    gain_s[...] = jnp.broadcast_to(gain[...], (8, D))
    down_pipe, up_pipe = (prv, i), (nxt, i)
    ship = [
        remote(meta_s.at[0], meta_r.at[0], xs.at[0], xr.at[0], down_pipe),
        remote(gain_s, gain_r, xs.at[1], xr.at[1], down_pipe),
        remote(xin.at[0], shp.at[0], xs.at[2], xr.at[2], down_pipe),
        remote(xin.at[1], shp.at[1], xs.at[3], xr.at[3], down_pipe),
        remote(meta_s.at[1], meta_r.at[1], xs.at[4], xr.at[4], up_pipe),
        remote(xin.at[2], shp.at[2], xs.at[5], xr.at[5], up_pipe),
    ]
    for c in ship:
        c.start()

    PAIR, OWN = 0, PART

    def source(n):
        return (z - FAR[n] + NZ) % NZ

    def row_sets(part, gs):
        pos, nb = span(gs)
        return pl.ds(part + 16 * pos, 16 * nb), pl.ds(part + T + 16 * gs[0], 16 * len(gs))

    def first(j, part, gs, mats, unfolded=False):
        src = recv if part else pair
        pos, nb = span(gs)
        e0 = 16 * NG if part else 0
        es = slice(e0 + 16 * gs[0], e0 + 16 * (gs[-1] + 1))

        def blocks(lo, n, ds):
            return [src[j, source(m), :, ds] for m in range(lo, lo + n)]

        if not unfolded:
            for g in gs:
                folded = jnp.concatenate(blocks(*GROUP[g], slice(D, W)), axis=0)
                for k in range(4):
                    extra[j, e0 + 16 * g:e0 + 16 * (g + 1), k * C:(k + 1) * C] = dot_nn(
                        unfold(k, GROUP[g][1]), folded).astype(BF16)
        at, at_ex = row_sets(part, gs)
        for m, _, _ in mats:
            acc[m, at] = jnp.zeros((16 * nb, H), F32)
            acc[m, at_ex] = jnp.zeros((16 * len(gs), H), F32)

        def step(n, _):
            ds = pl.ds(pl.multiple_of(n * KC, KC), KC)
            v = jnp.concatenate(blocks(pos, nb, ds) + [extra[j, es, ds]], axis=0)
            for m, w, transposed in mats:
                o = dot_nt(v, w[:, ds]) if transposed else dot_nn(v, w[ds, :])
                acc[m, at] += o[:16 * nb]
                acc[m, at_ex] += o[16 * nb:]
            return 0

        lax.fori_loop(0, NK, step, 0)

    def have_pair(j, gs):
        relay_all(j, span(gs)[1], gs[0]).wait_recv()

    gate_up = [(2, gate_o, False), (3, gate_r, False), (4, up_o, False), (5, up_r, False)]
    downs = [(0, down_o, True), (1, down_r, True)]

    def act(fn, part, gs):
        at, at_ex = row_sets(part, gs)

        def step(n, _):
            fn(pl.ds(pl.multiple_of(at.start + n * 16, 16), 16))
            return 0

        lax.fori_loop(0, at.size // 16, step, 0)
        fn(at_ex)

    def act_fwd(ds):
        for s in range(2):
            pg, pu = acc[2 + s, ds], acc[4 + s, ds]
            hid[s, ds] = (pg * jax.nn.sigmoid(pg) * pu).astype(BF16)

    def act_back(ds):
        for s in range(2):
            dh, pg, pu = acc[s, ds], acc[2 + s, ds], acc[4 + s, ds]
            sg = jax.nn.sigmoid(pg)
            hid[2 + s, ds] = (dh * pu * sg * (1.0 + pg * (1.0 - sg))).astype(BF16)
            hid[4 + s, ds] = (dh * pg * sg).astype(BF16)

    def out_rows(b, part, gs, ds):
        at, at_ex = row_sets(part, gs)
        h = [jnp.concatenate([hid[n, at], hid[n, at_ex]], axis=0) for n in ((2, 3, 4, 5) if b == 0 else (0, 1))]
        if b == 1:
            return dot_nn(h[0], down_o[:, ds]) + dot_nn(h[1], down_r[:, ds])
        return (dot_nt(h[0], gate_o[ds, :]) + dot_nt(h[1], gate_r[ds, :])
                + dot_nt(h[2], up_o[ds, :]) + dot_nt(h[3], up_r[ds, :]))

    def cols(n):
        return pl.ds(n * KC, KC) if isinstance(n, int) else pl.ds(pl.multiple_of(n * KC, KC), KC)

    def part_copy(b, gs, n):
        ds = pl.ds(D, C) if isinstance(n, int) and n == NK else cols(n)
        at, h = pl.ds(*span(gs)), 0 if b else 1 + gs[0]
        return remote(part_s.at[b, at, :, ds], part_r.at[b, at, :, ds], ps.at[b], pr.at[h, n], tok)

    def fold_extra(dst, b, gs):
        for g in gs:
            pos, nb = GROUP[g]
            folded = jnp.zeros((16 * nb, C), F32)
            for k in range(4):
                folded = folded + dot_nn(fold(k, nb), eo_b[16 * g:16 * (g + 1), k * C:(k + 1) * C])
            dst[b, pos:pos + nb, :, D:] = folded.astype(BF16).reshape(nb, 16, C)

    def theirs(b, gs, n):
        pos, nb = span(gs)
        ds = cols(n)
        o = out_rows(b, PAIR, gs, ds).astype(BF16)
        part_s[b, pos:pos + nb, :, ds] = o[:16 * nb].reshape(nb, 16, KC)
        eo_b[16 * gs[0]:16 * (gs[-1] + 1), ds] = o[16 * nb:]
        part_copy(b, gs, n).start()

    def theirs_extra(b, gs):
        fold_extra(part_s, b, gs)
        part_copy(b, gs, NK).start()

    def ours(b, gs, n):
        pos, nb = span(gs)
        ds = cols(n)
        o = out_rows(b, OWN, gs, ds)
        own[b, 16 * pos:16 * (pos + nb), ds] = o[:16 * nb]
        eo_f[b, 16 * gs[0]:16 * (gs[-1] + 1), ds] = o[16 * nb:]

    def ret_copy(b, g, n):
        ds = pl.ds(*COLS[g])
        return remote(ret_s.at[b, n, :, ds], ret_r.at[b, n, :, ds], rs.at[b],
                      rr.at[2 if b else n // GROUP[-1][0]], at_z(prv if b == 0 else nxt, source(n)))

    def ret_all(b, nb, h):
        at = pl.ds(0, nb)
        return remote(ret_s.at[b, at], ret_r.at[b, at], rs.at[b], rr.at[h], at_z(prv if b == 0 else nxt, z))

    def ret_send(b, gs, g):
        pos, nb = span(gs)
        for n in range(pos, pos + nb):
            ret_copy(b, g, n).start()

    def add(b, gs, n):
        pos, nb = span(gs)
        ds = cols(n)
        part_copy(b, gs, n).wait_recv()
        o = own[b, 16 * pos:16 * (pos + nb), ds] + part_r[b, pos:pos + nb, :, ds].reshape(16 * nb, KC).astype(F32)
        ret_s[b, pos:pos + nb, :, ds] = o.astype(BF16).reshape(nb, 16, KC)
        if n % 2 == 1:
            ret_send(b, gs, n // 2)

    def add_extra(b, gs):
        part_copy(b, gs, NK).wait_recv()
        for g in gs:
            pos, nb = GROUP[g]
            at = slice(16 * g, 16 * (g + 1))
            folded = part_r[b, pos:pos + nb, :, D:].reshape(16 * nb, C)
            for k in range(4):
                ks = slice(k * C, (k + 1) * C)
                eo_b[at, ks] = (eo_f[b, at, ks] + dot_nn(unfold(k, nb), folded)).astype(BF16)
        fold_extra(ret_s, b, gs)
        ret_send(b, gs, 3)

    def repeat(fn, b, gs):
        def step(n, _):
            fn(b, gs, n)
            return 0

        lax.fori_loop(0, NK, step, 0)

    def grad_rows(g):
        have_pair(0, (g,))
        first(0, PAIR, (g,), downs)

    def gate_rows(g):
        first(1, PAIR, (g,), gate_up)
        act(act_back, PAIR, (g,))

    def names(g):
        return FAR[GROUP[g][0]:GROUP[g][0] + GROUP[g][1]]

    early = span((0, 1))[1]

    def make_picks():
        for c in ship:
            c.wait()
        for b in range(2):
            main = jnp.transpose(placing(meta_r[b, 0:1, :])).astype(BF16)
            for k in range(4):
                ex = jnp.transpose(placing(meta_r[b, 1:2, :] + 4.0 * k)).astype(BF16)
                pick0[b, k] = jnp.concatenate([main[:, :16 * early], ex[:, :16 * early]], axis=1)
                pick1[b, k] = jnp.concatenate([main[:, 16 * early:], ex[:, 16 * early:]], axis=1)

    for d in (0,) + NEAR:
        if d:
            z_copy(2, d).wait_recv()
        relay(2, (d,))
    keep(2).wait()
    loads[4].wait()
    loads[5].wait()
    loads[3].wait()
    weight_copies[0].wait_recv()
    weight_copies[1].wait_recv()
    first(2, OWN, ALL, gate_up)
    act(act_fwd, OWN, ALL)
    have_pair(2, ALL)
    first(2, PAIR, ALL, gate_up)
    act(act_fwd, PAIR, ALL)
    z_all(0).wait_recv()
    keep(0).wait()
    first(0, OWN, ALL, downs[:1])
    weight_copies[2].wait_recv()
    repeat(theirs, 1, ALL)
    theirs_extra(1, ALL)
    for n in range(2):
        ours(1, ALL, n)
        add(1, ALL, n)
    relay(0, names(0))
    z_all(1).wait_recv()
    relay(1, names(0))
    for n in range(2, 4):
        ours(1, ALL, n)
        add(1, ALL, n)
    first(0, OWN, ALL, downs[1:], True)
    for n in range(4, 6):
        ours(1, ALL, n)
        add(1, ALL, n)
    relay(0, names(1))
    keep(1).wait()
    first(1, OWN, ALL, gate_up)
    ours(1, ALL, 6)
    add(1, ALL, 6)
    add_extra(1, ALL)
    act(act_back, OWN, ALL)
    repeat(ours, 0, ALL)
    grad_rows(0)
    have_pair(1, (0,))
    gate_rows(0)
    repeat(theirs, 0, (0,))
    theirs_extra(0, (0,))
    relay(1, names(1))
    relay(0, names(2))
    relay(1, names(2))
    add(0, (0,), 0)
    add(0, (0,), 1)
    grad_rows(1)
    for n in range(2, NK):
        add(0, (0,), n)
    add_extra(0, (0,))
    make_picks()
    have_pair(1, (1,))
    gate_rows(1)
    repeat(theirs, 0, (1,))
    theirs_extra(0, (1,))
    grad_rows(2)
    for n in range(4):
        add(0, (1,), n)
    have_pair(1, (2,))
    gate_rows(2)
    for n in range(NK):
        theirs(0, (2,), n)
        if n == 1:
            for m in range(4, NK):
                add(0, (1,), m)
            add_extra(0, (1,))
    theirs_extra(0, (2,))
    for n in range(NK):
        add(0, (2,), n)
    add_extra(0, (2,))

    def take(b, pick, pos, nb, k):
        at = pl.ds(pos, nb)
        return dot_nn(pick[b, k], jnp.concatenate([
            ret_r[b, at, :, k * C:(k + 1) * C].reshape(16 * nb, C), ret_r[b, at, :, D:].reshape(16 * nb, C)], axis=0))

    def take0(b, k):
        return take(b, pick0, 0, early, k)

    def take1(b, k):
        return take(b, pick1, early, NZ - early, k)

    share_fwd = column(meta_r[1, 2:3, :])
    r = inv_rms(shp.at[1])
    ret_all(1, NZ, 2).wait_recv()
    for k in range(4):
        ks = slice(k * C, (k + 1) * C)
        outs[1, :, ks] = (shp[2, :, ks].astype(F32) + share_fwd * (take0(1, k) + take1(1, k))).astype(BF16)
    out_f = pltpu.make_async_copy(outs.at[1], nf.at[0], osem.at[0])
    out_f.start()

    ret_all(0, early, 0).wait_recv()
    for k in range(4):
        qbuf[:, k * C:(k + 1) * C] = take0(0, k)
    for j in range(3):
        z_all(j).wait_send()
        relay_all(j, NZ, 0).wait_send()
        weight_copies[j].wait_send()
    for b in range(2):
        remote(part_s.at[b], part_r.at[b], ps.at[b], pr.at[0, 0], tok).wait_send()
        ret_all(b, NZ, 0).wait_send()
    ret_all(0, NZ - early, 1).wait_recv()
    total = jnp.zeros((T, 1), F32)
    for k in range(4):
        ks = slice(k * C, (k + 1) * C)
        q = gain_r[0:1, ks] * (qbuf[:, ks] + take1(0, k))
        qbuf[:, ks] = q
        total = total + jnp.sum(shp[1, :, ks].astype(F32) * q, axis=1, keepdims=True)
    coef = r * r * r * (total / D)
    for k in range(4):
        ks = slice(k * C, (k + 1) * C)
        outs[0, :, ks] = (
            shp[0, :, ks].astype(F32) + (r * qbuf[:, ks] - shp[1, :, ks].astype(F32) * coef)).astype(BF16)
        pltpu.make_async_copy(outs.at[0, :, pl.ds(k * C, C)], nb.at[0, :, pl.ds(k * C, C)], osem.at[1]).start()

    out_f.wait()
    pltpu.make_async_copy(outs.at[0], nb.at[0], osem.at[1]).wait()


def settle(nf, nb, nf_out, nb_out, held, sem_in, sem_out):
    into, out = [], []
    for n, (src, dst) in enumerate(((nf, nf_out), (nb, nb_out))):
        for m in range(4):
            at = pl.ds(32 * m, 32)
            into.append(pltpu.make_async_copy(src.at[0, at], held.at[n, at], sem_in.at[n, m]))
            out.append(pltpu.make_async_copy(held.at[n, at], dst.at[0, at], sem_out.at[n, m]))
    for c in into:
        c.start()
    for c, d in zip(into, out):
        c.wait()
        d.start()
    for d in out:
        d.wait()


def per_device(fin, froute, fshare, bin_, bgrad, broute, bshare, gain, gate, up, down):
    vm = pl.BlockSpec(memory_space=pltpu.VMEM)
    hbm = pl.BlockSpec(memory_space=pl.ANY)
    dma = pltpu.SemaphoreType.DMA
    out = jax.ShapeDtypeStruct((1, T, D), BF16)
    v = pltpu.VMEM
    nf, nb = pl.pallas_call(
        kernel,
        out_shape=(out, out),
        in_specs=[hbm, vm, vm, hbm, hbm, vm, vm, vm, hbm, hbm, hbm],
        out_specs=(hbm, hbm),
        scratch_shapes=[
            v((3, T, D), BF16), v((3, T, D), BF16), v((2, 8, T), F32), v((2, 8, T), F32),
            v((8, D), F32), v((8, D), F32),
            v((3, NZ, 16, W), BF16), v((3, NZ, 16, W), BF16), v((3, NZ, 16, W), BF16), v((3, 32 * NG, D), BF16),
            v((D, H), BF16), v((D, H), BF16), v((H, D), BF16),
            v((D, H), BF16), v((D, H), BF16), v((H, D), BF16),
            v((6, 2 * PART, H), F32), v((6, 2 * PART, H), BF16),
            v((2, NZ, 16, W), BF16), v((2, NZ, 16, W), BF16),
            v((2, T, D), F32), v((16 * NG, D), BF16), v((2, 16 * NG, D), F32),
            v((2, NZ, 16, W), BF16), v((2, NZ, 16, W), BF16), v((T, D), F32),
            v((2, 4, T, 192), BF16), v((2, 4, T, 64), BF16), v((2, T, D), BF16),
            dma((9,)), dma((3,)), dma((2,)), dma((NZ,)), dma((3,)), dma((3, NG)),
            dma((3,)), dma((3,)), dma((2,)), dma((1 + NG, NK + 1)),
            dma((2,)), dma((3,)), dma((6,)), dma((6,)), dma((2,)),
        ],
        compiler_params=pltpu.CompilerParams(
            collective_id=1, has_side_effects=True, vmem_limit_bytes=60 << 20
        ),
        name="dualpipe_step",
    )(
        fin, froute.reshape(1, T), fshare.reshape(1, T), bin_, bgrad, broute.reshape(1, T),
        bshare.reshape(1, T), gain, gate, up, down,
    )
    return pl.pallas_call(
        settle,
        out_shape=(out, out),
        in_specs=[pl.BlockSpec(memory_space=pltpu.HBM)] * 2,
        out_specs=(hbm, hbm),
        scratch_shapes=[v((2, T, D), BF16), dma((2, 4)), dma((2, 4))],
        compiler_params=pltpu.CompilerParams(vmem_limit_bytes=60 << 20),
        name="settle",
    )(nf, nb)


def solution(mesh):
    spec = P("pipe", "expert", None)
    return jax.shard_map(
        per_device,
        mesh=mesh,
        in_specs=(
            spec, spec, spec, spec, spec, spec, spec,
            P("pipe", None), P("pipe", None, "expert"), P("pipe", None, "expert"), P("pipe", "expert", None),
        ),
        out_specs=(spec, spec),
        check_vma=False,
    )
```

```python
import jax
import jax.numpy as jnp
from jax import lax
from jax.experimental import pallas as pl
from jax.experimental.pallas import tpu as pltpu
from jax.sharding import PartitionSpec as P

MESH = pl.DeviceIdType.MESH
NP, NZ, NY = 8, 8, 4
T = 128
D = 3584
C = 896
W = D + C
H = 256
KC = 512
NK = D // KC
F32, BF16 = jnp.float32, jnp.bfloat16
ORDER = (4, 3, 5, 2, 6, 1, 7)
NEAR = (1, 7, 2, 6, 3, 5, 4)
FAR = (4, 3, 5, 2, 6, 1, 7, 0)
COLS = ((0, 512), (512, 1024), (1536, 1024), (2560, 1024), (3584, 896))
GROUP = ((0, 3), (3, 3), (6, 2))
NG = len(GROUP)
ALL = tuple(range(NG))
PART = T + 16 * NG


def span(gs):
    return GROUP[gs[0]][0], sum(GROUP[g][1] for g in gs)


def dot_nn(a, b):
    return lax.dot_general(a, b, (((1,), (0,)), ((), ())), preferred_element_type=F32)


def dot_nt(a, b):
    return lax.dot_general(a, b, (((1,), (1,)), ((), ())), preferred_element_type=F32)


def iota(shape, dim):
    return lax.broadcasted_iota(jnp.int32, shape, dim)


def slots_of(route_row, z):
    onehot = (iota((16, T), 0) == route_row).astype(F32)
    before = (iota((T, T), 0) < iota((T, T), 1)).astype(F32).astype(BF16)
    count = dot_nn(onehot.astype(BF16), before)
    rank = jnp.sum(count * onehot, axis=0, keepdims=True)
    place = jnp.zeros_like(rank)
    for n, d in enumerate(FAR):
        place = place + jnp.where(route_row == (z + d) % NZ, float(n), 0.0)
    slots = []
    for base in (route_row.astype(F32) * 16.0, place * 16.0):
        slots.append(jnp.where(rank < 15.5, base + rank, -1000.0))
        slots.append(jnp.where(rank < 15.5, -1000.0, base + rank - 16.0))
    return slots


def placing(slot_row):
    return (iota((T, T), 0).astype(F32) == slot_row).astype(F32)


def column(row):
    return jnp.transpose(jnp.broadcast_to(row, (T, T)))[:, 0:1]


def unfold(k, nb):
    m, n = iota((16, 16 * nb), 0), iota((16, 16 * nb), 1)
    return (n == (m >> 2) * 16 + (m & 3) + 4 * k).astype(F32).astype(BF16)


def fold(k, nb):
    n, m = iota((16 * nb, 16), 0), iota((16 * nb, 16), 1)
    return (n == (m >> 2) * 16 + (m & 3) + 4 * k).astype(F32).astype(BF16)


def kernel(
    fin, froute, fshare, bin_, bgrad, broute, bshare, gain, gate, up, down,
    nf, nb,
    xin, shp, meta_s, meta_r, gain_s, gain_r, send, recv, pair, extra,
    gate_o, up_o, down_o, gate_r, up_r, down_r,
    acc, hid, part_s, part_r, own, eo_b, eo_f, own_ex, ret_s, ret_r, qbuf, pick0, pick1,
    lsem, zs, zr, zrf, ys, yr, ws, wr, ps, pr, rs, rr, xs, xr,
):
    p = lax.axis_index("pipe")
    i = lax.axis_index("expert")
    z, y = i // NY, i % NY
    core = p % 2
    nxt, prv = (p + 1) % NP, (p + NP - 1) % NP
    ya = y + 1 - 2 * (y % 2)
    yb = (y + NY - 1 + 2 * (y % 2)) % NY
    yt = ya * (1 - core) + yb * core
    yw = ya * core + yb * (1 - core)

    def at_z(pp, zz):
        return (pp, zz * NY + y)

    tok = (p, z * NY + yt)
    wgt = (p, z * NY + yw)

    def remote(src, dst, s, r, device):
        return pltpu.make_async_remote_copy(
            src_ref=src, dst_ref=dst, send_sem=s, recv_sem=r, device_id=device, device_id_type=MESH
        )

    loads = [
        pltpu.make_async_copy(bgrad.at[0], xin.at[0], lsem.at[0]),
        pltpu.make_async_copy(bin_.at[0], xin.at[1], lsem.at[1]),
        pltpu.make_async_copy(fin.at[0], xin.at[2], lsem.at[2]),
        pltpu.make_async_copy(down.at[0], down_o, lsem.at[3]),
        pltpu.make_async_copy(gate.at[0], gate_o, lsem.at[4]),
        pltpu.make_async_copy(up.at[0], up_o, lsem.at[5]),
    ]
    for n in (2, 0, 1, 4, 5, 3):
        loads[n].start()

    bar = pltpu.get_barrier_semaphore()

    def greet(d, _):
        pl.semaphore_signal(bar, inc=1, device_id=at_z(nxt, (z + d) % NZ), device_id_type=MESH)
        pl.semaphore_signal(bar, inc=1, device_id=at_z(prv, (z + d) % NZ), device_id_type=MESH)
        return 0

    def greet_own(d, _):
        pl.semaphore_signal(bar, inc=1, device_id=at_z(p, (z + d) % NZ), device_id_type=MESH)
        return 0

    lax.fori_loop(0, NZ, greet, 0)
    lax.fori_loop(1, NZ, greet_own, 0)
    pl.semaphore_signal(bar, inc=1, device_id=tok, device_id_type=MESH)
    pl.semaphore_signal(bar, inc=1, device_id=wgt, device_id_type=MESH)

    def pack(j, main, ex, chunk):
        pm = placing(main).astype(BF16)
        folded = jnp.zeros((T, C), F32)
        for k in range(4):
            v = chunk(k)
            send[j, :, :, k * C:(k + 1) * C] = dot_nn(pm, v).astype(BF16).reshape(NZ, 16, C)
            folded = folded + dot_nn(placing(ex + 4.0 * k).astype(BF16), v)
        send[j, :, :, D:] = folded.astype(BF16).reshape(NZ, 16, C)

    def inv_rms(ref):
        total = jnp.zeros((T, 1), F32)
        for k in range(4):
            v = ref[:, k * C:(k + 1) * C].astype(F32)
            total = total + jnp.sum(v * v, axis=1, keepdims=True)
        return lax.rsqrt(total / D + 1e-6)

    def pack_normed(j, main, ex):
        loads[j].wait()
        r = inv_rms(xin.at[j])
        pack(j, main, ex, lambda k: (
            xin[j, :, k * C:(k + 1) * C].astype(F32) * r * gain[:, k * C:(k + 1) * C]).astype(BF16))

    def z_copy(j, d):
        return remote(send.at[j, (z + d) % NZ], recv.at[j, z], zs.at[j],
                      zrf.at[d] if j == 2 else zr.at[j], at_z(p, (z + d) % NZ))

    def z_all(j):
        return remote(send.at[j, pl.ds(0, 7)], recv.at[j, pl.ds(0, 7)], zs.at[j], zr.at[j % 2], tok)

    def relay_copy(j, d):
        src = (z - d + NZ) % NZ
        ref = send.at[j, src] if d == 0 else recv.at[j, src]
        g = 0
        if j < 2:
            g = [d in FAR[lo:lo + nb] for lo, nb in GROUP].index(True)
        return remote(ref, pair.at[j, src], ys.at[j], yr.at[j, g], tok)

    def relay_all(j, nb, g):
        return remote(recv.at[j, pl.ds(0, nb)], pair.at[j, pl.ds(0, nb)], ys.at[j], yr.at[j, g], tok)

    def relay(j, ds):
        for d in ds:
            relay_copy(j, d).start()

    def keep(j):
        return pltpu.make_async_copy(send.at[j, z], recv.at[j, z], lsem.at[6 + j])

    def z_send(j):
        for d in ORDER:
            z_copy(j, d).start()
        keep(j).start()

    weight_copies = [
        remote(gate.at[0], gate_r, ws.at[0], wr.at[0], wgt),
        remote(up.at[0], up_r, ws.at[1], wr.at[1], wgt),
        remote(down.at[0], down_r, ws.at[2], wr.at[2], wgt),
    ]

    fmain, fextra, ftake, ftake_ex = slots_of(froute[...], z)
    pack_normed(2, fmain, fextra)
    pl.semaphore_wait(bar, 25)
    for c in weight_copies:
        c.start()
    z_send(2)

    bmain, bextra, btake, btake_ex = slots_of(broute[...], z)
    loads[0].wait()
    share_col = column(bshare[...])
    pack(0, bmain, bextra, lambda k: (share_col * xin[0, :, k * C:(k + 1) * C].astype(F32)).astype(BF16))
    z_send(0)
    pack_normed(1, bmain, bextra)
    z_send(1)

    def rows(*parts):
        return jnp.concatenate(list(parts) + [jnp.zeros((8 - len(parts), T), F32)], axis=0)

    meta_s[0] = rows(btake, btake_ex)
    meta_s[1] = rows(ftake, ftake_ex, fshare[...])
    gain_s[...] = jnp.broadcast_to(gain[...], (8, D))
    down_pipe, up_pipe = (prv, i), (nxt, i)
    ship = [
        remote(meta_s.at[0], meta_r.at[0], xs.at[0], xr.at[0], down_pipe),
        remote(gain_s, gain_r, xs.at[1], xr.at[1], down_pipe),
        remote(xin.at[0], shp.at[0], xs.at[2], xr.at[2], down_pipe),
        remote(xin.at[1], shp.at[1], xs.at[3], xr.at[3], down_pipe),
        remote(meta_s.at[1], meta_r.at[1], xs.at[4], xr.at[4], up_pipe),
        remote(xin.at[2], shp.at[2], xs.at[5], xr.at[5], up_pipe),
    ]
    for c in ship:
        c.start()

    PAIR, OWN = 0, PART

    def source(n):
        return (z - FAR[n] + NZ) % NZ

    def row_sets(part, gs):
        pos, nb = span(gs)
        return pl.ds(part + 16 * pos, 16 * nb), pl.ds(part + T + 16 * gs[0], 16 * len(gs))

    def first(j, part, gs, mats, unfolded=False):
        src = recv if part else pair
        pos, nb = span(gs)
        e0 = 16 * NG if part else 0
        es = slice(e0 + 16 * gs[0], e0 + 16 * (gs[-1] + 1))

        def blocks(lo, n, ds):
            return [src[j, source(m), :, ds] for m in range(lo, lo + n)]

        if not unfolded:
            for g in gs:
                folded = jnp.concatenate(blocks(*GROUP[g], slice(D, W)), axis=0)
                for k in range(4):
                    extra[j, e0 + 16 * g:e0 + 16 * (g + 1), k * C:(k + 1) * C] = dot_nn(
                        unfold(k, GROUP[g][1]), folded).astype(BF16)
        at, at_ex = row_sets(part, gs)
        for m, _, _ in mats:
            acc[m, at] = jnp.zeros((16 * nb, H), F32)
            acc[m, at_ex] = jnp.zeros((16 * len(gs), H), F32)

        def step(n, _):
            ds = pl.ds(pl.multiple_of(n * KC, KC), KC)
            v = jnp.concatenate(blocks(pos, nb, ds) + [extra[j, es, ds]], axis=0)
            for m, w, transposed in mats:
                o = dot_nt(v, w[:, ds]) if transposed else dot_nn(v, w[ds, :])
                acc[m, at] += o[:16 * nb]
                acc[m, at_ex] += o[16 * nb:]
            return 0

        lax.fori_loop(0, NK, step, 0)

    def have_pair(j, gs):
        relay_all(j, span(gs)[1], gs[0]).wait_recv()

    gate_up = [(2, gate_o, False), (3, gate_r, False), (4, up_o, False), (5, up_r, False)]
    downs = [(0, down_o, True), (1, down_r, True)]

    def act(fn, part, gs):
        at, at_ex = row_sets(part, gs)

        def step(n, _):
            fn(pl.ds(pl.multiple_of(at.start + n * 16, 16), 16))
            return 0

        lax.fori_loop(0, at.size // 16, step, 0)
        fn(at_ex)

    def act_fwd(ds):
        for s in range(2):
            pg, pu = acc[2 + s, ds], acc[4 + s, ds]
            hid[s, ds] = (pg * jax.nn.sigmoid(pg) * pu).astype(BF16)

    def act_back(ds):
        for s in range(2):
            dh, pg, pu = acc[s, ds], acc[2 + s, ds], acc[4 + s, ds]
            sg = jax.nn.sigmoid(pg)
            hid[2 + s, ds] = (dh * pu * sg * (1.0 + pg * (1.0 - sg))).astype(BF16)
            hid[4 + s, ds] = (dh * pg * sg).astype(BF16)

    def out_rows(b, part, gs, ds):
        at, at_ex = row_sets(part, gs)
        h = [jnp.concatenate([hid[n, at], hid[n, at_ex]], axis=0) for n in ((2, 3, 4, 5) if b == 0 else (0, 1))]
        if b == 1:
            return dot_nn(h[0], down_o[:, ds]) + dot_nn(h[1], down_r[:, ds])
        return (dot_nt(h[0], gate_o[ds, :]) + dot_nt(h[1], gate_r[ds, :])
                + dot_nt(h[2], up_o[ds, :]) + dot_nt(h[3], up_r[ds, :]))

    def cols(n):
        return pl.ds(n * KC, KC) if isinstance(n, int) else pl.ds(pl.multiple_of(n * KC, KC), KC)

    def part_copy(b, gs, n):
        ds = pl.ds(D, C) if isinstance(n, int) and n == NK else cols(n)
        at, h = pl.ds(*span(gs)), 0 if b else 1 + gs[0]
        return remote(part_s.at[b, at, :, ds], part_r.at[b, at, :, ds], ps.at[b], pr.at[h, n], tok)

    def fold_extra(b, gs):
        for g in gs:
            pos, nb = GROUP[g]
            folded = jnp.zeros((16 * nb, C), F32)
            for k in range(4):
                folded = folded + dot_nn(fold(k, nb), eo_b[16 * g:16 * (g + 1), k * C:(k + 1) * C])
            part_s[b, pos:pos + nb, :, D:] = folded.astype(BF16).reshape(nb, 16, C)

    def theirs(b, gs, n):
        pos, nb = span(gs)
        ds = cols(n)
        o = out_rows(b, PAIR, gs, ds).astype(BF16)
        part_s[b, pos:pos + nb, :, ds] = o[:16 * nb].reshape(nb, 16, KC)
        eo_b[16 * gs[0]:16 * (gs[-1] + 1), ds] = o[16 * nb:]
        part_copy(b, gs, n).start()

    def theirs_extra(b, gs):
        fold_extra(b, gs)
        part_copy(b, gs, NK).start()

    def ours(b, gs, n):
        pos, nb = span(gs)
        ds = cols(n)
        o = out_rows(b, OWN, gs, ds)
        own[b, 16 * pos:16 * (pos + nb), ds] = o[:16 * nb]
        eo_f[b, 16 * gs[0]:16 * (gs[-1] + 1), ds] = o[16 * nb:]

    def ret_copy(b, g, n):
        ds = pl.ds(*COLS[g])
        return remote(ret_s.at[b, n, :, ds], ret_r.at[b, n, :, ds], rs.at[b],
                      rr.at[2 if b else min(n // GROUP[0][1], 1)], at_z(prv if b == 0 else nxt, source(n)))

    def ret_all(b, nb, h):
        at = pl.ds(0, nb)
        return remote(ret_s.at[b, at], ret_r.at[b, at], rs.at[b], rr.at[h], at_z(prv if b == 0 else nxt, z))

    def ret_send(b, gs, g):
        pos, nb = span(gs)
        for n in range(pos, pos + nb):
            ret_copy(b, g, n).start()

    def add(b, gs, n):
        pos, nb = span(gs)
        ds = cols(n)
        part_copy(b, gs, n).wait_recv()
        o = own[b, 16 * pos:16 * (pos + nb), ds] + part_r[b, pos:pos + nb, :, ds].reshape(16 * nb, KC).astype(F32)
        ret_s[b, pos:pos + nb, :, ds] = o.astype(BF16).reshape(nb, 16, KC)
        if n % 2 == 0:
            ret_send(b, gs, n // 2)

    def fold_own(b):
        for g, (pos, nb) in enumerate(GROUP):
            for m in range(nb):
                for k in range(4):
                    own_ex[b, 16 * (pos + m) + 4 * k:16 * (pos + m) + 4 * (k + 1), :] = (
                        eo_f[b, 16 * g + 4 * m:16 * g + 4 * (m + 1), k * C:(k + 1) * C])

    def add_extra(b, gs):
        pos, nb = span(gs)
        part_copy(b, gs, NK).wait_recv()
        o = own_ex[b, 16 * pos:16 * (pos + nb)] + part_r[b, pos:pos + nb, :, D:].reshape(16 * nb, C).astype(F32)
        ret_s[b, pos:pos + nb, :, D:] = o.astype(BF16).reshape(nb, 16, C)
        ret_send(b, gs, 4)

    def repeat(fn, b, gs):
        def step(n, _):
            fn(b, gs, n)
            return 0

        lax.fori_loop(0, NK, step, 0)

    def grad_rows(g):
        have_pair(0, (g,))
        first(0, PAIR, (g,), downs)

    def gate_rows(g):
        first(1, PAIR, (g,), gate_up)
        act(act_back, PAIR, (g,))

    def names(g):
        return FAR[GROUP[g][0]:GROUP[g][0] + GROUP[g][1]]

    early = GROUP[0][1]

    def make_picks():
        for c in ship:
            c.wait()
        for b in range(2):
            main = jnp.transpose(placing(meta_r[b, 0:1, :])).astype(BF16)
            for k in range(4):
                ex = jnp.transpose(placing(meta_r[b, 1:2, :] + 4.0 * k)).astype(BF16)
                pick0[b, k] = jnp.concatenate([main[:, :16 * early], ex[:, :16 * early]], axis=1)
                pick1[b, k] = jnp.concatenate([main[:, 16 * early:], ex[:, 16 * early:]], axis=1)

    for d in (0,) + NEAR:
        if d:
            z_copy(2, d).wait_recv()
        relay(2, (d,))
    keep(2).wait()
    loads[4].wait()
    loads[5].wait()
    loads[3].wait()
    weight_copies[0].wait_recv()
    weight_copies[1].wait_recv()
    first(2, OWN, ALL, gate_up)
    act(act_fwd, OWN, ALL)
    have_pair(2, ALL)
    first(2, PAIR, ALL, gate_up)
    act(act_fwd, PAIR, ALL)
    z_all(0).wait_recv()
    keep(0).wait()
    first(0, OWN, ALL, downs[:1])
    weight_copies[2].wait_recv()
    repeat(theirs, 1, ALL)
    theirs_extra(1, ALL)
    for n in range(2):
        ours(1, ALL, n)
        add(1, ALL, n)
    relay(0, names(0))
    z_all(1).wait_recv()
    relay(1, names(0))
    for n in range(2, 4):
        ours(1, ALL, n)
        add(1, ALL, n)
    first(0, OWN, ALL, downs[1:], True)
    for n in range(4, 6):
        ours(1, ALL, n)
        add(1, ALL, n)
    relay(0, names(1))
    keep(1).wait()
    first(1, OWN, ALL, gate_up)
    ours(1, ALL, 6)
    fold_own(1)
    add(1, ALL, 6)
    add_extra(1, ALL)
    act(act_back, OWN, ALL)
    repeat(ours, 0, ALL)
    fold_own(0)
    grad_rows(0)
    have_pair(1, (0,))
    gate_rows(0)
    for n in range(NK):
        theirs(0, (0,), n)
        if n == 5:
            add(0, (0,), 0)
    theirs_extra(0, (0,))
    relay(1, names(1))
    relay(0, names(2))
    relay(1, names(2))
    for n in range(1, 3):
        add(0, (0,), n)
    grad_rows(1)
    for n in range(3, NK):
        add(0, (0,), n)
    add_extra(0, (0,))
    make_picks()
    have_pair(1, (1,))
    gate_rows(1)
    repeat(theirs, 0, (1,))
    theirs_extra(0, (1,))
    grad_rows(2)
    for n in range(4):
        add(0, (1,), n)
    have_pair(1, (2,))
    gate_rows(2)
    for n in range(NK):
        theirs(0, (2,), n)
        if n == 1:
            for m in range(4, NK):
                add(0, (1,), m)
            add_extra(0, (1,))
    theirs_extra(0, (2,))
    for n in range(NK):
        add(0, (2,), n)
    add_extra(0, (2,))

    def take(b, pick, pos, nb, k):
        at = pl.ds(pos, nb)
        return dot_nn(pick[b, k], jnp.concatenate([
            ret_r[b, at, :, k * C:(k + 1) * C].reshape(16 * nb, C), ret_r[b, at, :, D:].reshape(16 * nb, C)], axis=0))

    def take0(b, k):
        return take(b, pick0, 0, early, k)

    def take1(b, k):
        return take(b, pick1, early, NZ - early, k)

    share_fwd = column(meta_r[1, 2:3, :])
    r = inv_rms(shp.at[1])
    ret_all(1, NZ, 2).wait_recv()
    for k in range(4):
        ks = slice(k * C, (k + 1) * C)
        nf[0, :, ks] = (shp[2, :, ks].astype(F32) + share_fwd * (take0(1, k) + take1(1, k))).astype(BF16)

    ret_all(0, early, 0).wait_recv()
    for k in range(4):
        qbuf[:, k * C:(k + 1) * C] = take0(0, k)
    for j in range(3):
        z_all(j).wait_send()
        relay_all(j, NZ, 0).wait_send()
        weight_copies[j].wait_send()
    for b in range(2):
        remote(part_s.at[b], part_r.at[b], ps.at[b], pr.at[0, 0], tok).wait_send()
        ret_all(b, NZ, 0).wait_send()
    ret_all(0, NZ - early, 1).wait_recv()
    total = jnp.zeros((T, 1), F32)
    for k in range(4):
        ks = slice(k * C, (k + 1) * C)
        q = gain_r[0:1, ks] * (qbuf[:, ks] + take1(0, k))
        qbuf[:, ks] = q
        total = total + jnp.sum(shp[1, :, ks].astype(F32) * q, axis=1, keepdims=True)
    coef = r * r * r * (total / D)
    for k in range(4):
        ks = slice(k * C, (k + 1) * C)
        nb[0, :, ks] = (
            shp[0, :, ks].astype(F32) + (r * qbuf[:, ks] - shp[1, :, ks].astype(F32) * coef)).astype(BF16)


def per_device(fin, froute, fshare, bin_, bgrad, broute, bshare, gain, gate, up, down):
    vm = pl.BlockSpec(memory_space=pltpu.VMEM)
    hbm = pl.BlockSpec(memory_space=pl.ANY)
    dma = pltpu.SemaphoreType.DMA
    v = pltpu.VMEM
    return pl.pallas_call(
        kernel,
        out_shape=(v((1, T, D), BF16), v((1, T, D), BF16)),
        in_specs=[hbm, vm, vm, hbm, hbm, vm, vm, vm, hbm, hbm, hbm],
        out_specs=(vm, vm),
        scratch_shapes=[
            v((3, T, D), BF16), v((3, T, D), BF16), v((2, 8, T), F32), v((2, 8, T), F32),
            v((8, D), F32), v((8, D), F32),
            v((3, NZ, 16, W), BF16), v((3, NZ, 16, W), BF16), v((3, NZ, 16, W), BF16), v((3, 32 * NG, D), BF16),
            v((D, H), BF16), v((D, H), BF16), v((H, D), BF16),
            v((D, H), BF16), v((D, H), BF16), v((H, D), BF16),
            v((6, 2 * PART, H), F32), v((6, 2 * PART, H), BF16),
            v((2, NZ, 16, W), BF16), v((2, NZ, 16, W), BF16),
            v((2, T, D), F32), v((16 * NG, D), BF16), v((2, 16 * NG, D), F32), v((2, T, C), F32),
            v((2, NZ, 16, W), BF16), v((2, NZ, 16, W), BF16), v((T, D), F32),
            v((2, 4, T, 96), BF16), v((2, 4, T, 160), BF16),
            dma((9,)), dma((3,)), dma((2,)), dma((NZ,)), dma((3,)), dma((3, NG)),
            dma((3,)), dma((3,)), dma((2,)), dma((1 + NG, NK + 1)),
            dma((2,)), dma((3,)), dma((6,)), dma((6,)),
        ],
        compiler_params=pltpu.CompilerParams(
            collective_id=1, has_side_effects=True, vmem_limit_bytes=60 << 20
        ),
        name="dualpipe_step",
    )(
        fin, froute.reshape(1, T), fshare.reshape(1, T), bin_, bgrad, broute.reshape(1, T),
        bshare.reshape(1, T), gain, gate, up, down,
    )


def solution(mesh):
    spec = P("pipe", "expert", None)
    return jax.shard_map(
        per_device,
        mesh=mesh,
        in_specs=(
            spec, spec, spec, spec, spec, spec, spec,
            P("pipe", None), P("pipe", None, "expert"), P("pipe", None, "expert"), P("pipe", "expert", None),
        ),
        out_specs=(spec, spec),
        check_vma=False,
    )
```

```python
import jax
import jax.numpy as jnp
from jax import lax
from jax.experimental import pallas as pl
from jax.experimental.pallas import tpu as pltpu
from jax.sharding import PartitionSpec as P

MESH = pl.DeviceIdType.MESH
NP, NZ, NY = 8, 8, 4
T = 128
D = 3584
C = 896
W = D + C
H = 256
KC = 512
NK = D // KC
K1 = 1792
F32, BF16 = jnp.float32, jnp.bfloat16
ORDER = (4, 3, 5, 2, 6, 1, 7)
NEAR = (1, 7, 2, 6, 3, 5, 4)
FAR = (4, 3, 5, 2, 6, 1, 7, 0)
COLS = ((0, 512), (512, 1024), (1536, 1024), (2560, 1024), (3584, 896))
GROUP = ((0, 3), (3, 3), (6, 2))
NG = len(GROUP)
ALL = tuple(range(NG))
PART = T + 16 * NG


def span(gs):
    return GROUP[gs[0]][0], sum(GROUP[g][1] for g in gs)


def dot_nn(a, b):
    return lax.dot_general(a, b, (((1,), (0,)), ((), ())), preferred_element_type=F32)


def dot_nt(a, b):
    return lax.dot_general(a, b, (((1,), (1,)), ((), ())), preferred_element_type=F32)


def iota(shape, dim):
    return lax.broadcasted_iota(jnp.int32, shape, dim)


def slots_of(route_row, z):
    onehot = (iota((16, T), 0) == route_row).astype(F32)
    before = (iota((T, T), 0) < iota((T, T), 1)).astype(F32).astype(BF16)
    count = dot_nn(onehot.astype(BF16), before)
    rank = jnp.sum(count * onehot, axis=0, keepdims=True)
    place = jnp.zeros_like(rank)
    for n, d in enumerate(FAR):
        place = place + jnp.where(route_row == (z + d) % NZ, float(n), 0.0)
    slots = []
    for base in (route_row.astype(F32) * 16.0, place * 16.0):
        slots.append(jnp.where(rank < 15.5, base + rank, -1000.0))
        slots.append(jnp.where(rank < 15.5, -1000.0, base + rank - 16.0))
    return slots


def placing(slot_row):
    return (iota((T, T), 0).astype(F32) == slot_row).astype(F32)


def column(row):
    return jnp.transpose(jnp.broadcast_to(row, (T, T)))[:, 0:1]


def unfold(k, nb):
    m, n = iota((16, 16 * nb), 0), iota((16, 16 * nb), 1)
    return (n == (m >> 2) * 16 + (m & 3) + 4 * k).astype(F32).astype(BF16)


def fold(k, nb):
    n, m = iota((16 * nb, 16), 0), iota((16 * nb, 16), 1)
    return (n == (m >> 2) * 16 + (m & 3) + 4 * k).astype(F32).astype(BF16)


def kernel(
    fin, froute, fshare, bin_, bgrad, broute, bshare, gain, gate, up, down,
    nf, nb,
    xin, shp, meta_s, meta_r, gain_s, gain_r, send, recv, pair, extra,
    gate_o, up_o, down_o, gate_r, up_r, down_r,
    acc, hid, part_s, part_r, own, eo_b, eo_f, own_ex, ret_s, ret_r, qbuf, pick0, pick1,
    lsem, zs, zr, zrf, ys, yr, ws, wr, ps, pr, rs, rr, xs, xr,
):
    p = lax.axis_index("pipe")
    i = lax.axis_index("expert")
    z, y = i // NY, i % NY
    core = p % 2
    nxt, prv = (p + 1) % NP, (p + NP - 1) % NP
    ya = y + 1 - 2 * (y % 2)
    yb = (y + NY - 1 + 2 * (y % 2)) % NY
    yt = ya * (1 - core) + yb * core
    yw = ya * core + yb * (1 - core)

    def at_z(pp, zz):
        return (pp, zz * NY + y)

    tok = (p, z * NY + yt)
    wgt = (p, z * NY + yw)

    def remote(src, dst, s, r, device):
        return pltpu.make_async_remote_copy(
            src_ref=src, dst_ref=dst, send_sem=s, recv_sem=r, device_id=device, device_id_type=MESH
        )

    loads = [
        pltpu.make_async_copy(bgrad.at[0], xin.at[0], lsem.at[0]),
        pltpu.make_async_copy(bin_.at[0], xin.at[1], lsem.at[1]),
        pltpu.make_async_copy(fin.at[0], xin.at[2], lsem.at[2]),
        pltpu.make_async_copy(down.at[0], down_o, lsem.at[3]),
        pltpu.make_async_copy(gate.at[0], gate_o, lsem.at[4]),
        pltpu.make_async_copy(up.at[0], up_o, lsem.at[5]),
    ]
    for n in (2, 0, 1, 4, 5, 3):
        loads[n].start()

    bar = pltpu.get_barrier_semaphore()

    def greet(d, _):
        pl.semaphore_signal(bar, inc=1, device_id=at_z(nxt, (z + d) % NZ), device_id_type=MESH)
        pl.semaphore_signal(bar, inc=1, device_id=at_z(prv, (z + d) % NZ), device_id_type=MESH)
        return 0

    def greet_own(d, _):
        pl.semaphore_signal(bar, inc=1, device_id=at_z(p, (z + d) % NZ), device_id_type=MESH)
        return 0

    lax.fori_loop(0, NZ, greet, 0)
    lax.fori_loop(1, NZ, greet_own, 0)
    pl.semaphore_signal(bar, inc=1, device_id=tok, device_id_type=MESH)
    pl.semaphore_signal(bar, inc=1, device_id=wgt, device_id_type=MESH)

    def pack(j, main, ex, chunk):
        pm = placing(main).astype(BF16)
        folded = jnp.zeros((T, C), F32)
        for k in range(4):
            v = chunk(k)
            send[j, :, :, k * C:(k + 1) * C] = dot_nn(pm, v).astype(BF16).reshape(NZ, 16, C)
            folded = folded + dot_nn(placing(ex + 4.0 * k).astype(BF16), v)
        send[j, :, :, D:] = folded.astype(BF16).reshape(NZ, 16, C)

    def inv_rms(ref):
        total = jnp.zeros((T, 1), F32)
        for k in range(4):
            v = ref[:, k * C:(k + 1) * C].astype(F32)
            total = total + jnp.sum(v * v, axis=1, keepdims=True)
        return lax.rsqrt(total / D + 1e-6)

    def pack_normed(j, main, ex):
        loads[j].wait()
        r = inv_rms(xin.at[j])
        pack(j, main, ex, lambda k: (
            xin[j, :, k * C:(k + 1) * C].astype(F32) * r * gain[:, k * C:(k + 1) * C]).astype(BF16))

    def z_copy(j, d):
        return remote(send.at[j, (z + d) % NZ], recv.at[j, z], zs.at[j],
                      zrf.at[d] if j == 2 else zr.at[j], at_z(p, (z + d) % NZ))

    def z_all(j):
        return remote(send.at[j, pl.ds(0, 7)], recv.at[j, pl.ds(0, 7)], zs.at[j], zr.at[j % 2], tok)

    def relay_copy(j, d):
        src = (z - d + NZ) % NZ
        ref = send.at[j, src] if d == 0 else recv.at[j, src]
        g = 0
        if j < 2:
            g = [d in FAR[lo:lo + nb] for lo, nb in GROUP].index(True)
        return remote(ref, pair.at[j, src], ys.at[j], yr.at[j, g], tok)

    def relay_all(j, nb, g):
        return remote(recv.at[j, pl.ds(0, nb)], pair.at[j, pl.ds(0, nb)], ys.at[j], yr.at[j, g], tok)

    def relay(j, ds):
        for d in ds:
            relay_copy(j, d).start()

    def keep(j):
        return pltpu.make_async_copy(send.at[j, z], recv.at[j, z], lsem.at[6 + j])

    def z_send(j):
        for d in ORDER:
            z_copy(j, d).start()
        keep(j).start()

    weight_copies = [
        remote(gate.at[0], gate_r, ws.at[0], wr.at[0], wgt),
        remote(up.at[0], up_r, ws.at[1], wr.at[1], wgt),
        remote(down.at[0], down_r, ws.at[2], wr.at[2], wgt),
    ]

    fmain, fextra, ftake, ftake_ex = slots_of(froute[...], z)
    pack_normed(2, fmain, fextra)
    pl.semaphore_wait(bar, 25)
    for c in weight_copies:
        c.start()
    z_send(2)

    bmain, bextra, btake, btake_ex = slots_of(broute[...], z)
    loads[0].wait()
    share_col = column(bshare[...])
    pack(0, bmain, bextra, lambda k: (share_col * xin[0, :, k * C:(k + 1) * C].astype(F32)).astype(BF16))
    z_send(0)
    pack_normed(1, bmain, bextra)
    z_send(1)

    def rows(*parts):
        return jnp.concatenate(list(parts) + [jnp.zeros((8 - len(parts), T), F32)], axis=0)

    meta_s[0] = rows(btake, btake_ex)
    meta_s[1] = rows(ftake, ftake_ex, fshare[...])
    gain_s[...] = jnp.broadcast_to(gain[...], (8, D))
    down_pipe, up_pipe = (prv, i), (nxt, i)
    ship = [
        remote(meta_s.at[0], meta_r.at[0], xs.at[0], xr.at[0], down_pipe),
        remote(gain_s, gain_r, xs.at[1], xr.at[1], down_pipe),
        remote(xin.at[0], shp.at[0], xs.at[2], xr.at[2], down_pipe),
        remote(xin.at[1], shp.at[1], xs.at[3], xr.at[3], down_pipe),
        remote(meta_s.at[1], meta_r.at[1], xs.at[4], xr.at[4], up_pipe),
        remote(xin.at[2], shp.at[2], xs.at[5], xr.at[5], up_pipe),
    ]
    for c in ship:
        c.start()

    PAIR, OWN = 0, PART

    def source(n):
        return (z - FAR[n] + NZ) % NZ

    def row_sets(part, gs):
        pos, nb = span(gs)
        return pl.ds(part + 16 * pos, 16 * nb), pl.ds(part + T + 16 * gs[0], 16 * len(gs))

    def first(j, part, gs, mats, unfolded=False):
        src = recv if part else pair
        pos, nb = span(gs)
        e0 = 16 * NG if part else 0
        es = slice(e0 + 16 * gs[0], e0 + 16 * (gs[-1] + 1))

        def blocks(lo, n, ds):
            return [src[j, source(m), :, ds] for m in range(lo, lo + n)]

        if not unfolded:
            for g in gs:
                folded = jnp.concatenate(blocks(*GROUP[g], slice(D, W)), axis=0)
                for k in range(4):
                    extra[j, e0 + 16 * g:e0 + 16 * (g + 1), k * C:(k + 1) * C] = dot_nn(
                        unfold(k, GROUP[g][1]), folded).astype(BF16)
        at, at_ex = row_sets(part, gs)
        for m, _, _ in mats:
            acc[m, at] = jnp.zeros((16 * nb, H), F32)
            acc[m, at_ex] = jnp.zeros((16 * len(gs), H), F32)

        def step(n, _):
            ds = pl.ds(pl.multiple_of(n * K1, K1), K1)
            v = jnp.concatenate(blocks(pos, nb, ds) + [extra[j, es, ds]], axis=0)
            for m, w, transposed in mats:
                o = dot_nt(v, w[:, ds]) if transposed else dot_nn(v, w[ds, :])
                acc[m, at] += o[:16 * nb]
                acc[m, at_ex] += o[16 * nb:]
            return 0

        lax.fori_loop(0, D // K1, step, 0)

    def have_pair(j, gs):
        relay_all(j, span(gs)[1], gs[0]).wait_recv()

    gate_up = [(2, gate_o, False), (3, gate_r, False), (4, up_o, False), (5, up_r, False)]
    downs = [(0, down_o, True), (1, down_r, True)]

    def act(fn, part, gs):
        at, at_ex = row_sets(part, gs)

        def step(n, _):
            fn(pl.ds(pl.multiple_of(at.start + n * 16, 16), 16))
            return 0

        lax.fori_loop(0, at.size // 16, step, 0)
        fn(at_ex)

    def act_fwd(ds):
        for s in range(2):
            pg, pu = acc[2 + s, ds], acc[4 + s, ds]
            hid[s, ds] = (pg * jax.nn.sigmoid(pg) * pu).astype(BF16)

    def act_back(ds):
        for s in range(2):
            dh, pg, pu = acc[s, ds], acc[2 + s, ds], acc[4 + s, ds]
            sg = jax.nn.sigmoid(pg)
            hid[2 + s, ds] = (dh * pu * sg * (1.0 + pg * (1.0 - sg))).astype(BF16)
            hid[4 + s, ds] = (dh * pg * sg).astype(BF16)

    def out_rows(b, part, gs, ds):
        at, at_ex = row_sets(part, gs)
        h = [jnp.concatenate([hid[n, at], hid[n, at_ex]], axis=0) for n in ((2, 3, 4, 5) if b == 0 else (0, 1))]
        if b == 1:
            return dot_nn(h[0], down_o[:, ds]) + dot_nn(h[1], down_r[:, ds])
        return (dot_nt(h[0], gate_o[ds, :]) + dot_nt(h[1], gate_r[ds, :])
                + dot_nt(h[2], up_o[ds, :]) + dot_nt(h[3], up_r[ds, :]))

    def cols(n):
        return pl.ds(n * KC, KC) if isinstance(n, int) else pl.ds(pl.multiple_of(n * KC, KC), KC)

    def part_copy(b, gs, n):
        ds = pl.ds(D, C) if isinstance(n, int) and n == NK else cols(n)
        at, h = pl.ds(*span(gs)), 0 if b else 1 + gs[0]
        return remote(part_s.at[b, at, :, ds], part_r.at[b, at, :, ds], ps.at[b], pr.at[h, n], tok)

    def fold_extra(b, gs):
        for g in gs:
            pos, nb = GROUP[g]
            folded = jnp.zeros((16 * nb, C), F32)
            for k in range(4):
                folded = folded + dot_nn(fold(k, nb), eo_b[16 * g:16 * (g + 1), k * C:(k + 1) * C])
            part_s[b, pos:pos + nb, :, D:] = folded.astype(BF16).reshape(nb, 16, C)

    def theirs(b, gs, n):
        pos, nb = span(gs)
        ds = cols(n)
        o = out_rows(b, PAIR, gs, ds).astype(BF16)
        part_s[b, pos:pos + nb, :, ds] = o[:16 * nb].reshape(nb, 16, KC)
        eo_b[16 * gs[0]:16 * (gs[-1] + 1), ds] = o[16 * nb:]
        part_copy(b, gs, n).start()

    def theirs_extra(b, gs):
        fold_extra(b, gs)
        part_copy(b, gs, NK).start()

    def ours(b, gs, n):
        pos, nb = span(gs)
        ds = cols(n)
        o = out_rows(b, OWN, gs, ds)
        own[b, 16 * pos:16 * (pos + nb), ds] = o[:16 * nb]
        eo_f[b, 16 * gs[0]:16 * (gs[-1] + 1), ds] = o[16 * nb:]

    def ret_copy(b, g, n):
        ds = pl.ds(*COLS[g])
        return remote(ret_s.at[b, n, :, ds], ret_r.at[b, n, :, ds], rs.at[b],
                      rr.at[2 if b else min(n // GROUP[0][1], 1)], at_z(prv if b == 0 else nxt, source(n)))

    def ret_all(b, nb, h):
        at = pl.ds(0, nb)
        return remote(ret_s.at[b, at], ret_r.at[b, at], rs.at[b], rr.at[h], at_z(prv if b == 0 else nxt, z))

    def ret_send(b, gs, g):
        pos, nb = span(gs)
        for n in range(pos, pos + nb):
            ret_copy(b, g, n).start()

    def add(b, gs, n):
        pos, nb = span(gs)
        ds = cols(n)
        part_copy(b, gs, n).wait_recv()
        o = own[b, 16 * pos:16 * (pos + nb), ds] + part_r[b, pos:pos + nb, :, ds].reshape(16 * nb, KC).astype(F32)
        ret_s[b, pos:pos + nb, :, ds] = o.astype(BF16).reshape(nb, 16, KC)
        if n % 2 == 0:
            ret_send(b, gs, n // 2)

    def fold_own(b):
        for g, (pos, nb) in enumerate(GROUP):
            for m in range(nb):
                for k in range(4):
                    own_ex[b, 16 * (pos + m) + 4 * k:16 * (pos + m) + 4 * (k + 1), :] = (
                        eo_f[b, 16 * g + 4 * m:16 * g + 4 * (m + 1), k * C:(k + 1) * C])

    def add_extra(b, gs):
        pos, nb = span(gs)
        part_copy(b, gs, NK).wait_recv()
        o = own_ex[b, 16 * pos:16 * (pos + nb)] + part_r[b, pos:pos + nb, :, D:].reshape(16 * nb, C).astype(F32)
        ret_s[b, pos:pos + nb, :, D:] = o.astype(BF16).reshape(nb, 16, C)
        ret_send(b, gs, 4)

    def repeat(fn, b, gs):
        def step(n, _):
            fn(b, gs, n)
            return 0

        lax.fori_loop(0, NK, step, 0)

    def grad_rows(g):
        have_pair(0, (g,))
        first(0, PAIR, (g,), downs)

    def gate_rows(g):
        first(1, PAIR, (g,), gate_up)
        act(act_back, PAIR, (g,))

    def names(g):
        return FAR[GROUP[g][0]:GROUP[g][0] + GROUP[g][1]]

    early = GROUP[0][1]

    def make_picks():
        for c in ship:
            c.wait()
        for b in range(2):
            main = jnp.transpose(placing(meta_r[b, 0:1, :])).astype(BF16)
            for k in range(4):
                ex = jnp.transpose(placing(meta_r[b, 1:2, :] + 4.0 * k)).astype(BF16)
                pick0[b, k] = jnp.concatenate([main[:, :16 * early], ex[:, :16 * early]], axis=1)
                pick1[b, k] = jnp.concatenate([main[:, 16 * early:], ex[:, 16 * early:]], axis=1)

    for d in (0,) + NEAR:
        if d:
            z_copy(2, d).wait_recv()
        relay(2, (d,))
    keep(2).wait()
    loads[4].wait()
    loads[5].wait()
    loads[3].wait()
    weight_copies[0].wait_recv()
    weight_copies[1].wait_recv()
    first(2, OWN, ALL, gate_up)
    act(act_fwd, OWN, ALL)
    have_pair(2, ALL)
    first(2, PAIR, ALL, gate_up)
    act(act_fwd, PAIR, ALL)
    z_all(0).wait_recv()
    keep(0).wait()
    first(0, OWN, ALL, downs[:1])
    weight_copies[2].wait_recv()
    repeat(theirs, 1, ALL)
    theirs_extra(1, ALL)
    for n in range(2):
        ours(1, ALL, n)
        add(1, ALL, n)
    relay(0, names(0))
    z_all(1).wait_recv()
    relay(1, names(0))
    for n in range(2, 4):
        ours(1, ALL, n)
        add(1, ALL, n)
    first(0, OWN, ALL, downs[1:], True)
    for n in range(4, 6):
        ours(1, ALL, n)
        add(1, ALL, n)
    relay(0, names(1))
    keep(1).wait()
    first(1, OWN, ALL, gate_up)
    ours(1, ALL, 6)
    fold_own(1)
    add(1, ALL, 6)
    add_extra(1, ALL)
    act(act_back, OWN, ALL)
    repeat(ours, 0, ALL)
    fold_own(0)
    grad_rows(0)
    have_pair(1, (0,))
    gate_rows(0)
    for n in range(NK):
        theirs(0, (0,), n)
        if n == 5:
            add(0, (0,), 0)
    theirs_extra(0, (0,))
    relay(1, names(1))
    relay(0, names(2))
    relay(1, names(2))
    for n in range(1, 3):
        add(0, (0,), n)
    grad_rows(1)
    for n in range(3, NK):
        add(0, (0,), n)
    add_extra(0, (0,))
    make_picks()
    have_pair(1, (1,))
    gate_rows(1)
    repeat(theirs, 0, (1,))
    theirs_extra(0, (1,))
    grad_rows(2)
    for n in range(4):
        add(0, (1,), n)
    have_pair(1, (2,))
    gate_rows(2)
    for n in range(NK):
        theirs(0, (2,), n)
        if n == 1:
            for m in range(4, NK):
                add(0, (1,), m)
            add_extra(0, (1,))
    theirs_extra(0, (2,))
    for n in range(NK):
        add(0, (2,), n)
    add_extra(0, (2,))

    def take(b, pick, pos, nb, k):
        at = pl.ds(pos, nb)
        return dot_nn(pick[b, k], jnp.concatenate([
            ret_r[b, at, :, k * C:(k + 1) * C].reshape(16 * nb, C), ret_r[b, at, :, D:].reshape(16 * nb, C)], axis=0))

    def take0(b, k):
        return take(b, pick0, 0, early, k)

    def take1(b, k):
        return take(b, pick1, early, NZ - early, k)

    share_fwd = column(meta_r[1, 2:3, :])
    r = inv_rms(shp.at[1])
    ret_all(1, NZ, 2).wait_recv()
    for k in range(4):
        ks = slice(k * C, (k + 1) * C)
        nf[0, :, ks] = (shp[2, :, ks].astype(F32) + share_fwd * (take0(1, k) + take1(1, k))).astype(BF16)

    ret_all(0, early, 0).wait_recv()
    for k in range(4):
        qbuf[:, k * C:(k + 1) * C] = take0(0, k)
    for j in range(3):
        z_all(j).wait_send()
        relay_all(j, NZ, 0).wait_send()
        weight_copies[j].wait_send()
    for b in range(2):
        remote(part_s.at[b], part_r.at[b], ps.at[b], pr.at[0, 0], tok).wait_send()
        ret_all(b, NZ, 0).wait_send()
    ret_all(0, NZ - early, 1).wait_recv()
    total = jnp.zeros((T, 1), F32)
    for k in range(4):
        ks = slice(k * C, (k + 1) * C)
        q = gain_r[0:1, ks] * (qbuf[:, ks] + take1(0, k))
        qbuf[:, ks] = q
        total = total + jnp.sum(shp[1, :, ks].astype(F32) * q, axis=1, keepdims=True)
    coef = r * r * r * (total / D)
    for k in range(4):
        ks = slice(k * C, (k + 1) * C)
        nb[0, :, ks] = (
            shp[0, :, ks].astype(F32) + (r * qbuf[:, ks] - shp[1, :, ks].astype(F32) * coef)).astype(BF16)


def per_device(fin, froute, fshare, bin_, bgrad, broute, bshare, gain, gate, up, down):
    vm = pl.BlockSpec(memory_space=pltpu.VMEM)
    hbm = pl.BlockSpec(memory_space=pl.ANY)
    dma = pltpu.SemaphoreType.DMA
    v = pltpu.VMEM
    return pl.pallas_call(
        kernel,
        out_shape=(v((1, T, D), BF16), v((1, T, D), BF16)),
        in_specs=[hbm, vm, vm, hbm, hbm, vm, vm, vm, hbm, hbm, hbm],
        out_specs=(vm, vm),
        scratch_shapes=[
            v((3, T, D), BF16), v((3, T, D), BF16), v((2, 8, T), F32), v((2, 8, T), F32),
            v((8, D), F32), v((8, D), F32),
            v((3, NZ, 16, W), BF16), v((3, NZ, 16, W), BF16), v((3, NZ, 16, W), BF16), v((3, 32 * NG, D), BF16),
            v((D, H), BF16), v((D, H), BF16), v((H, D), BF16),
            v((D, H), BF16), v((D, H), BF16), v((H, D), BF16),
            v((6, 2 * PART, H), F32), v((6, 2 * PART, H), BF16),
            v((2, NZ, 16, W), BF16), v((2, NZ, 16, W), BF16),
            v((2, T, D), F32), v((16 * NG, D), BF16), v((2, 16 * NG, D), F32), v((2, T, C), F32),
            v((2, NZ, 16, W), BF16), v((2, NZ, 16, W), BF16), v((T, D), F32),
            v((2, 4, T, 96), BF16), v((2, 4, T, 160), BF16),
            dma((9,)), dma((3,)), dma((2,)), dma((NZ,)), dma((3,)), dma((3, NG)),
            dma((3,)), dma((3,)), dma((2,)), dma((1 + NG, NK + 1)),
            dma((2,)), dma((3,)), dma((6,)), dma((6,)),
        ],
        compiler_params=pltpu.CompilerParams(
            collective_id=1, has_side_effects=True, vmem_limit_bytes=60 << 20
        ),
        name="dualpipe_step",
    )(
        fin, froute.reshape(1, T), fshare.reshape(1, T), bin_, bgrad, broute.reshape(1, T),
        bshare.reshape(1, T), gain, gate, up, down,
    )


def solution(mesh):
    spec = P("pipe", "expert", None)
    return jax.shard_map(
        per_device,
        mesh=mesh,
        in_specs=(
            spec, spec, spec, spec, spec, spec, spec,
            P("pipe", None), P("pipe", None, "expert"), P("pipe", None, "expert"), P("pipe", "expert", None),
        ),
        out_specs=(spec, spec),
        check_vma=False,
    )
```
